512 devices in a mesh: row: 32 (over x, y), col: 16 (over z, core).
Axes of the slice: x: 4, y: 8, z: 8, core: 2. Of those that a mesh axis runs over, the one named last changes fastest.
Arguments:
- points: bfloat16 [32, 65536], P(None, ('row', 'col')), may hold values from -6 to 6
- inv_scale: float32 [32], replicated, may hold values from 0.3 to 0.6
- amplitude: float32 [1], replicated, may hold values from 0.5 to 1.5
- noise: float32 [65536], P(('row', 'col')), may hold values from 0.1 to 4.2
- targets: float32 [65536], P(('row', 'col')), may hold values from -6 to 6
- probe_seeds: int32 [65536], P(('row', 'col')), may hold values from 0 to 127
Outputs:
- solution: float32 [8, 65536], P(None, ('row', 'col'))
- residual: float32 [8, 65536], P(None, ('row', 'col'))
The draws below stay inside these ranges and needn't reach their ends.
All inputs are finite; a program needn't handle non-finite values.
Results may differ from the reference program's by a relative error of at most 0.0097.
Values may be sent and summed in bfloat16 or wider, within the bound.
A program may use at most 64 MiB of HBM per device.

```python
import math
import jax
import jax.numpy as jnp
from jax import lax

F = 32
RHS = 8
ITERS = 2
POINTS = 65536


def position_ramp(start, finish):
    place = jnp.arange(POINTS, dtype=jnp.float32) / float(POINTS)
    return start + (finish - start) * place


def draw_noise(key, part):
    key = jax.random.fold_in(key, 12)
    factor_key = jax.random.fold_in(key, 0)
    rough = jnp.exp(jax.random.uniform(factor_key, (POINTS,), jnp.float32, math.log(0.7), math.log(1.4)))
    level = jnp.exp(position_ramp(math.log(0.15), math.log(3.0)))
    return (level * rough).astype(jnp.float32)


def draw_targets(key, part):
    key = jax.random.fold_in(key, 11)
    values = jax.random.normal(key, (POINTS,), jnp.float32)
    ramp = position_ramp(-1.2, 0.6)
    return jnp.clip(values * jnp.exp(ramp), -6.0, 6.0).astype(jnp.float32)


def with_ends(drawn, rng, low, high):
    index_at = [jax.random.randint(jax.random.fold_in(rng, axis), (), 0, length) for axis, length in enumerate(drawn.shape)]
    main_axis = drawn.shape.index(max(drawn.shape))
    next_to = index_at[:main_axis] + [(index_at[main_axis] + 1) % drawn.shape[main_axis]] + index_at[main_axis + 1:]
    return drawn.at[tuple(index_at)].set(low).at[tuple(next_to)].set(high)


def levels(rng, extent, pieces, smallest, largest):
    gain, own = 1.0, jax.random.fold_in(rng, 6)
    for dim, blocks in pieces:
        draws = jnp.exp(jax.random.uniform(jax.random.fold_in(own, dim), (blocks,), jnp.float32, smallest / len(pieces), largest / len(pieces)))
        gain = gain * jnp.repeat(draws, extent[dim] // blocks).reshape([-1 if axis == dim else 1 for axis in range(len(extent))])
    return gain


def bell_draw(key, shape, deviation, limit, cuts=(), kind=jnp.bfloat16):
    entries = deviation * jax.random.normal(key, shape, jnp.float32)
    if cuts:
        entries = entries * levels(key, shape, cuts, -0.22, 0.18)
    return jnp.clip(entries, -limit, limit).astype(kind)


def setup_inputs(seed: int = 0) -> dict:
    key_of = jax.random.split(jax.random.key(seed), 7)
    points = bell_draw(key_of[0], (F, POINTS), 1.0, 6.0, ((1, 512),))
    inv_scale = jnp.clip(jnp.exp(jax.random.uniform(key_of[1], (F,), jnp.float32, math.log(0.3), math.log(0.6))), 0.3, 0.6)
    amplitude = jnp.clip(jax.random.uniform(key_of[2], (1,), jnp.float32, 0.5, 1.5), 0.5, 1.5)
    noise = draw_noise(jax.random.fold_in(key_of[6], 71), 0)
    targets = draw_targets(jax.random.fold_in(key_of[6], 71), 0)
    probe_seeds = with_ends(jax.random.randint(key_of[5], (POINTS,), 0, 128), jax.random.fold_in(key_of[5], 1), 0, 127).astype(jnp.int32)
    return dict(points=points, inv_scale=inv_scale, amplitude=amplitude, noise=noise, targets=targets, probe_seeds=probe_seeds)


def kernel_tile(row_points, row_norms, col_points, col_norms):
    products = lax.dot_general(row_points, col_points, (((0,), (0,)), ((), ())), preferred_element_type=jnp.float32)
    return jnp.exp(products - 0.5 * row_norms[:, None] - 0.5 * col_norms[None, :]).astype(jnp.bfloat16)


def square_norms(values_bf):
    values = values_bf.astype(jnp.float32)
    return jnp.sum(values * values, axis=0)


def build_rhs(targets, probe_seeds):
    powers = (2 ** jnp.arange(RHS - 1)).astype(jnp.int32)
    flags = (probe_seeds[None, :].astype(jnp.int32) // powers[:, None]) % 2
    probes = (1 - 2 * flags).astype(jnp.float32)
    return jnp.concatenate([targets[None, :].astype(jnp.float32), probes], axis=0)


def image_of(scaled, norms, low, amplitude, noise):
    total = scaled.shape[1]
    height = math.gcd(total, 1024)
    count = total // height

    def rows_of(index):
        start = (index * height).astype(jnp.int32)
        slab = lax.dynamic_slice_in_dim(scaled, start, height, 1)
        slab_norms = lax.dynamic_slice_in_dim(norms, start, height, 0)
        tile = kernel_tile(slab, slab_norms, scaled, norms)
        return lax.dot_general(low, tile, (((1,), (1,)), ((), ())), preferred_element_type=jnp.float32)

    parts = lax.map(rows_of, jnp.arange(count, dtype=jnp.int32))
    summed = jnp.transpose(parts, (1, 0, 2)).reshape(low.shape[0], total)
    return amplitude[0] * summed + noise[None, :] * low.astype(jnp.float32)


def reference(points, inv_scale, amplitude, noise, targets, probe_seeds):
    scaled = (points.astype(jnp.float32) * inv_scale[:, None]).astype(jnp.bfloat16)
    norms = square_norms(scaled)
    rhs = build_rhs(targets, probe_seeds)
    solution = jnp.zeros_like(rhs)
    residual = rhs
    direction = rhs
    norm_now = jnp.sum(residual * residual, axis=1)
    for step in range(ITERS):
        low = direction.astype(jnp.bfloat16)
        image = image_of(scaled, norms, low, amplitude, noise)
        curvature = jnp.sum(low.astype(jnp.float32) * image, axis=1)
        alpha = norm_now / curvature
        solution = solution + alpha[:, None] * direction
        residual = residual - alpha[:, None] * image
        if step + 1 < ITERS:
            norm_next = jnp.sum(residual * residual, axis=1)
            direction = residual + (norm_next / norm_now)[:, None] * direction
            norm_now = norm_next
    return solution, residual
```

```python
import jax
import jax.numpy as jnp
from jax import lax
from jax.experimental import pallas as pl
from jax.experimental.pallas import tpu as pltpu
from jax.sharding import PartitionSpec as P

MESH = pl.DeviceIdType.MESH
F = 32
RHS = 8
LANES = 128
F32 = jnp.float32
BF16 = jnp.bfloat16

ROWS = 48


def pieces(value):
    first = value.astype(BF16).astype(F32)
    rest = value - first
    second = rest.astype(BF16).astype(F32)
    return first, second, rest - second


def wait_bytes(ref, sem):
    pltpu.make_async_copy(ref, ref, sem).wait()


def body(nx, ny, nc, refs):
    (points, inv, amp, noise, targets, seeds, sol, res) = refs[:8]
    (msg, jbuf, ibuf, weights, tile, acc, rs1, msg2, j2, i2, sc1, scal1,
     send2, rs2, fin_msg, fin) = refs[8:24]
    (s_row, s_col, r_row, r_col, s_rs1, r_rs1, s_row2, s_col2, r_row2, r_col2,
     s_sc, r_sc, s_rs2, r_rs2, s_fin, r_fin) = refs[24:]
    nr = nx * ny
    rows_i = nc * LANES
    group = ny * LANES
    row = lax.axis_index("row")
    col = lax.axis_index("col")
    x = row // ny
    y = row % ny

    def row_peer(k):
        return ((x + k // ny) % nx) * ny + (y + k % ny) % ny

    def col_peer(k):
        return (col + k) % nc

    def to_rows(src, dst, send, recv):
        pltpu.make_async_copy(src, dst, recv).start()

        def go(k, carry):
            pltpu.make_async_remote_copy(
                src_ref=src, dst_ref=dst, send_sem=send, recv_sem=recv,
                device_id=(row_peer(k), col), device_id_type=MESH,
            ).start()
            return carry

        lax.fori_loop(1, nr, go, 0)

    def to_cols(src_of, dst, send, recv):
        pltpu.make_async_copy(src_of(col), dst, recv).start()

        def go(k, carry):
            peer = col_peer(k)
            pltpu.make_async_remote_copy(
                src_ref=src_of(peer), dst_ref=dst, send_sem=send, recv_sem=recv,
                device_id=(row, peer), device_id_type=MESH,
            ).start()
            return carry

        lax.fori_loop(1, nc, go, 0)

    barrier = pltpu.get_barrier_semaphore()

    def greet_row(k, carry):
        pl.semaphore_signal(barrier, inc=1, device_id=(row_peer(k), col), device_id_type=MESH)
        return carry

    def greet_col(k, carry):
        pl.semaphore_signal(barrier, inc=1, device_id=(row, col_peer(k)), device_id_type=MESH)
        return carry

    lax.fori_loop(1, nr, greet_row, 0)
    lax.fori_loop(1, nc, greet_col, 0)

    eye = lax.broadcasted_iota(jnp.int32, (F, F), 0) == lax.broadcasted_iota(jnp.int32, (F, F), 1)
    factor = jnp.sum(jnp.where(eye, inv[...], 0.0), axis=1, keepdims=True)
    scaled = (points[...].astype(F32) * factor).astype(BF16)
    values = scaled.astype(F32)
    norm = -0.5 * jnp.sum(values * values, axis=0, keepdims=True)
    n1, n2, n3 = pieces(norm)
    sub = lax.broadcasted_iota(jnp.int32, (RHS, LANES), 0)
    lane = lax.broadcasted_iota(jnp.int32, (RHS, LANES), 1)
    bits = (seeds[...] >> jnp.maximum(sub - 1, 0)) & 1
    v0 = jnp.where(sub == 0, targets[...], (1 - 2 * bits).astype(F32))
    low = v0.astype(BF16).astype(F32)
    lost = targets[...] - targets[...].astype(BF16).astype(F32)
    extra = jnp.where(sub == 0, n1, jnp.where(sub == 1, n2, jnp.where(sub == 2, n3,
            jnp.where(sub < 6, 1.0, jnp.where(sub == 6, lost, 0.0)))))
    msg[0:F, :] = scaled
    msg[F:ROWS, :] = jnp.concatenate([extra, low], axis=0).astype(BF16)

    pl.semaphore_wait(barrier, nr - 1 + nc - 1)
    to_cols(lambda peer: msg, ibuf.at[col], s_col, r_col)
    to_rows(msg, jbuf.at[row], s_row, r_row.at[x])

    wait_bytes(ibuf, r_col)
    for c in range(nc):
        part = slice(c * LANES, (c + 1) * LANES)
        weights[0:F, part] = ibuf[c, 0:F, :]
        tail = ibuf[c, F:ROWS, :].astype(F32)
        swapped = jnp.where(sub < 3, 1.0, jnp.where(sub < 6, jnp.roll(tail[0:RHS], 3, axis=0), 0.0))
        weights[F:ROWS, part] = jnp.concatenate([swapped, jnp.zeros_like(swapped)], axis=0).astype(BF16)

    acc[...] = jnp.zeros_like(acc)

    def first_pass(t, carry):
        g = (x + t) % nx
        slots = jbuf.at[pl.ds(g * ny, ny)]
        wait_bytes(slots, r_row.at[g])
        block = jnp.concatenate([jbuf[g * ny + k] for k in range(ny)], axis=1)
        inner = lax.dot_general(block, weights[...], (((0,), (0,)), ((), ())), preferred_element_type=F32)
        kern = jnp.exp(inner).astype(BF16)
        tile[pl.ds(pl.multiple_of(g * group, group), group), :] = kern
        acc[...] += jnp.dot(block[F:ROWS], kern, preferred_element_type=F32)
        return carry

    lax.fori_loop(0, nx, first_pass, 0)

    to_cols(lambda peer: acc.at[pl.ds(RHS, RHS), pl.ds(pl.multiple_of(peer * LANES, LANES), LANES)],
            rs1.at[col], s_rs1, r_rs1)
    scale = amp[...]
    shift = noise[...]
    wait_bytes(rs1, r_rs1)
    q1 = scale * jnp.sum(rs1[...], axis=0) + shift * low
    msg2[0:RHS, :] = q1
    msg2[RHS:2 * RHS, :] = jnp.where(
        lane == 0, jnp.sum(v0 * v0, axis=1, keepdims=True),
        jnp.where(lane == 1, jnp.sum(low * q1, axis=1, keepdims=True), 0.0))
    to_rows(msg2, j2.at[row], s_row2, r_row2.at[x])
    to_cols(lambda peer: msg2, i2.at[col], s_col2, r_col2)

    wait_bytes(rs1.at[pl.ds(0, nc - 1)], s_rs1)
    acc[...] = jnp.zeros_like(acc)

    def second_pass(t, total):
        g = (x + t) % nx
        wait_bytes(j2.at[pl.ds(g * ny, ny)], r_row2.at[g])
        parts = [j2[g * ny + k] for k in range(ny)]
        for part in parts:
            total = total + part[RHS:2 * RHS]
        value = jnp.concatenate([part[0:RHS] for part in parts], axis=1)
        high = value.astype(BF16).astype(F32)
        both = jnp.concatenate([high, value - high], axis=0).astype(BF16)
        acc[...] += jnp.dot(both, tile[pl.ds(pl.multiple_of(g * group, group), group), :],
                            preferred_element_type=F32)
        return total

    scal1[...] = lax.fori_loop(0, nx, second_pass, jnp.zeros((RHS, LANES), F32))
    to_cols(lambda peer: scal1, sc1.at[col], s_sc, r_sc)
    wait_bytes(i2, r_col2)
    wait_bytes(sc1, r_sc)
    sums1 = jnp.sum(sc1[...], axis=0)
    rr0 = sums1[:, 0:1]
    curve1 = sums1[:, 1:2]
    alpha1 = rr0 / curve1
    r1 = v0 - alpha1 * q1

    cross = jnp.zeros((RHS, LANES), F32)
    for c in range(nc):
        part = slice(c * LANES, (c + 1) * LANES)
        second = acc[0:RHS, part] + acc[RHS:2 * RHS, part]
        send2[c, 0:RHS, :] = second
        tail = ibuf[c, F:ROWS, :].astype(F32)
        mine = tail[RHS:2 * RHS] + jnp.where(sub == 0, tail[6:7], 0.0)
        cross = cross + (mine - alpha1 * i2[c, 0:RHS, :]) * second
    cross = scale * cross + shift * r1 * q1
    sums = jnp.where(
        lane == 0, jnp.sum(cross, axis=1, keepdims=True), jnp.where(
            lane == 1, jnp.sum(r1 * r1, axis=1, keepdims=True), jnp.where(
                lane == 2, jnp.sum(r1 * q1, axis=1, keepdims=True), 0.0)))
    for c in range(nc):
        send2[c, RHS:2 * RHS, :] = sums
    to_cols(lambda peer: send2.at[peer], rs2.at[col], s_rs2, r_rs2)
    wait_bytes(rs2, r_rs2)
    fin_msg[...] = jnp.sum(rs2[:, RHS:2 * RHS, :], axis=0)
    to_rows(fin_msg, fin.at[row], s_fin, r_fin)
    q2 = scale * jnp.sum(rs2[:, 0:RHS, :], axis=0) + shift * q1
    wait_bytes(fin, r_fin)
    sums2 = jnp.sum(fin[...], axis=0)
    r1q2, rr1, r1q1 = sums2[:, 0:1], sums2[:, 1:2], sums2[:, 2:3]
    beta = rr1 / rr0
    curve2 = (r1q1 - alpha1 * r1q2) + 2.0 * beta * r1q1 + beta * beta * curve1
    alpha2 = rr1 / curve2
    d2 = r1 + beta * v0
    image2 = (q1 - alpha1 * q2) + beta * q1
    sol[...] = alpha1 * v0 + alpha2 * d2
    res[...] = r1 - alpha2 * image2

    wait_bytes(ibuf.at[pl.ds(0, nc - 1)], s_col)
    wait_bytes(jbuf.at[pl.ds(0, nr - 1)], s_row)
    wait_bytes(j2.at[pl.ds(0, nr - 1)], s_row2)
    wait_bytes(i2.at[pl.ds(0, nc - 1)], s_col2)
    wait_bytes(sc1.at[pl.ds(0, nc - 1)], s_sc)
    wait_bytes(rs2.at[pl.ds(0, nc - 1)], s_rs2)
    wait_bytes(fin.at[pl.ds(0, nr - 1)], s_fin)


def solution(mesh):
    nr, nc = mesh.shape["row"], mesh.shape["col"]
    ny = 8 if nr % 8 == 0 else nr
    nx = nr // ny
    vmem = pl.BlockSpec(memory_space=pltpu.VMEM)
    dma = pltpu.SemaphoreType.DMA

    def shards(points, inv_scale, amplitude, noise, targets, probe_seeds):
        out = jax.ShapeDtypeStruct((RHS, LANES), F32)
        return pl.pallas_call(
            lambda *refs: body(nx, ny, nc, refs),
            out_shape=(out, out),
            in_specs=[vmem] * 6,
            out_specs=(vmem, vmem),
            scratch_shapes=[
                pltpu.VMEM((ROWS, LANES), BF16),
                pltpu.VMEM((nr, ROWS, LANES), BF16),
                pltpu.VMEM((nc, ROWS, LANES), BF16),
                pltpu.VMEM((ROWS, nc * LANES), BF16),
                pltpu.VMEM((nr * LANES, nc * LANES), BF16),
                pltpu.VMEM((2 * RHS, nc * LANES), F32),
                pltpu.VMEM((nc, RHS, LANES), F32),
                pltpu.VMEM((2 * RHS, LANES), F32),
                pltpu.VMEM((nr, 2 * RHS, LANES), F32),
                pltpu.VMEM((nc, 2 * RHS, LANES), F32),
                pltpu.VMEM((nc, RHS, LANES), F32),
                pltpu.VMEM((RHS, LANES), F32),
                pltpu.VMEM((nc, 2 * RHS, LANES), F32),
                pltpu.VMEM((nc, 2 * RHS, LANES), F32),
                pltpu.VMEM((RHS, LANES), F32),
                pltpu.VMEM((nr, RHS, LANES), F32),
                dma, dma, dma((nx,)), dma, dma, dma, dma, dma, dma((nx,)), dma,
                dma, dma, dma, dma, dma, dma,
            ],
            compiler_params=pltpu.CompilerParams(
                collective_id=0, has_side_effects=True, vmem_limit_bytes=48 * 2**20),
        )(points, inv_scale.reshape(1, F), amplitude.reshape(1, 1), noise.reshape(1, LANES),
          targets.reshape(1, LANES), probe_seeds.reshape(1, LANES))

    spec = P(("row", "col"))
    both = P(None, ("row", "col"))
    return jax.shard_map(
        shards, mesh=mesh, in_specs=(both, P(), P(), spec, spec, spec),
        out_specs=(both, both), check_vma=False)
```

```python
import jax
import jax.numpy as jnp
from jax import lax
from jax.experimental import pallas as pl
from jax.experimental.pallas import tpu as pltpu
from jax.sharding import PartitionSpec as P

MESH = pl.DeviceIdType.MESH
F = 32
TAIL = 16
ROWS = F + TAIL
RHS = 8
LANES = 128
F32 = jnp.float32
BF16 = jnp.bfloat16


def pieces(value):
    first = value.astype(BF16).astype(F32)
    rest = value - first
    second = rest.astype(BF16).astype(F32)
    return first, second, rest - second


def wait_bytes(ref, sem):
    pltpu.make_async_copy(ref, ref, sem).wait()


def body(nx, ny, nc, refs):
    (points_in, inv_in, amp_in, noise_in, targets_in, seeds_in, sol, res) = refs[:8]
    (points, inv, amp, noise, targets, seeds) = refs[8:14]
    (pts, aux, jp, ja, ip, ia, weights, v_i, tile, acc, rs1, s1_msg, s1_col, s1_sum, s1_row,
     q1_msg, j2, i2, out2, s2_msg, s2_col, rs2, s2_sum, s2_row) = refs[14:38]
    (in_sem, s_pc, s_pr, r_pc, r_pr, s_ac, s_ar, r_ac, r_ar, s_rs1, r_rs1, s_s1c, r_s1c, s_s1r, r_s1r,
     s_q1c, s_q1r, r_q1c, r_q1r, s_s2c, r_s2c, s_rs2, r_rs2, s_s2r, r_s2r) = refs[38:]
    nr = nx * ny
    group = ny * LANES
    row = lax.axis_index("row")
    col = lax.axis_index("col")
    x = row // ny
    y = row % ny

    def turn(t):
        return (t * (7 - t) // 2) % 4 if nx == 4 else t

    def row_peer(k):
        return ((x + nx - turn(k // ny)) % nx) * ny + (y + k % ny) % ny

    def col_peer(k):
        return (col + k) % nc

    def to_rows(*copies):
        for src, dst, send, recv in copies:
            pltpu.make_async_copy(src, dst, recv).start()

        def go(k, carry):
            peer = row_peer(k)
            for src, dst, send, recv in copies:
                pltpu.make_async_remote_copy(
                    src_ref=src, dst_ref=dst, send_sem=send, recv_sem=recv,
                    device_id=(peer, col), device_id_type=MESH,
                ).start()
            return carry

        lax.fori_loop(1, nr, go, 0)

    def to_cols(*copies):
        for src_of, dst, send, recv in copies:
            pltpu.make_async_copy(src_of(col), dst, recv).start()

        def go(k, carry):
            peer = col_peer(k)
            for src_of, dst, send, recv in copies:
                pltpu.make_async_remote_copy(
                    src_ref=src_of(peer), dst_ref=dst, send_sem=send, recv_sem=recv,
                    device_id=(row, peer), device_id_type=MESH,
                ).start()
            return carry

        lax.fori_loop(1, nc, go, 0)

    loads = [pltpu.make_async_copy(a, b, in_sem.at[n]) for n, (a, b) in enumerate((
        (points_in, points), (inv_in, inv), (targets_in, targets), (seeds_in, seeds),
        (noise_in, noise), (amp_in, amp)))]
    for load in loads:
        load.start()

    barrier = pltpu.get_barrier_semaphore()

    def greet_row(k, carry):
        pl.semaphore_signal(barrier, inc=1, device_id=(row_peer(k), col), device_id_type=MESH)
        return carry

    def greet_col(k, carry):
        pl.semaphore_signal(barrier, inc=1, device_id=(row, col_peer(k)), device_id_type=MESH)
        return carry

    lax.fori_loop(1, nr, greet_row, 0)
    lax.fori_loop(1, nc, greet_col, 0)

    sub = lax.broadcasted_iota(jnp.int32, (RHS, LANES), 0)
    lane = lax.broadcasted_iota(jnp.int32, (RHS, LANES), 1)

    def build_rhs(target, seed):
        bits = (seed.astype(jnp.int32) >> jnp.maximum(sub - 1, 0)) & 1
        return jnp.where(sub == 0, target, (1 - 2 * bits).astype(F32))

    def minus_half_norm(block):
        values = block.astype(F32)
        return -0.5 * jnp.sum(values * values, axis=0, keepdims=True)

    def as_row(sums):
        spread = jnp.zeros((RHS, LANES), F32)
        for q, value in enumerate(sums):
            spread = spread + jnp.where(lane == q * RHS + sub, value, 0.0)
        return jnp.sum(spread, axis=0, keepdims=True)

    def from_row(total, q):
        return jnp.sum(jnp.where(lane == q * RHS + sub, total, 0.0), axis=1, keepdims=True)

    def rowsum(value):
        return jnp.sum(value, axis=1, keepdims=True)

    for load in loads:
        load.wait()
    eye = lax.broadcasted_iota(jnp.int32, (F, F), 0) == lax.broadcasted_iota(jnp.int32, (F, F), 1)
    factor = jnp.sum(jnp.where(eye, inv[...], 0.0), axis=1, keepdims=True)
    pts[...] = (points[...].astype(F32) * factor).astype(BF16)
    aux[0:1, :] = targets[...]
    aux[1:2, :] = seeds[...].astype(F32)

    pl.semaphore_wait(barrier, nr - 1 + nc - 1)
    to_cols((lambda peer: aux, ia.at[col], s_ac, r_ac), (lambda peer: pts, ip.at[col], s_pc, r_pc))
    to_rows((aux, ja.at[row], s_ar, r_ar.at[x]), (pts, jp.at[row], s_pr, r_pr.at[x]))
    v0 = build_rhs(targets[...], seeds[...])
    low = v0.astype(BF16).astype(F32)
    scale = amp[...]
    shift = noise[...]
    acc[...] = jnp.zeros_like(acc)

    wait_bytes(ia, r_ac)
    wait_bytes(ip, r_pc)
    for c in range(nc):
        part = slice(c * LANES, (c + 1) * LANES)
        block = ip[c]
        n1, n2, n3 = pieces(minus_half_norm(block))
        weights[0:F, part] = block
        extra = jnp.where(sub < 3, 1.0, jnp.where(sub == 3, n1, jnp.where(sub == 4, n2, jnp.where(sub == 5, n3, 0.0))))
        weights[F:ROWS, part] = jnp.concatenate([extra, jnp.zeros_like(extra)], axis=0).astype(BF16)
        v_i[:, part] = build_rhs(ia[c, 0:1], ia[c, 1:2])

    def first_pass(t, carry):
        g = (x + turn(t)) % nx
        wait_bytes(ja.at[pl.ds(g * ny, ny)], r_ar.at[g])
        wait_bytes(jp.at[pl.ds(g * ny, ny)], r_pr.at[g])
        blocks, tails = [], []
        for k in range(ny):
            block = jp[g * ny + k]
            info = ja[g * ny + k]
            n1, n2, n3 = pieces(minus_half_norm(block))
            extra = jnp.where(sub == 0, n1, jnp.where(sub == 1, n2, jnp.where(sub == 2, n3, jnp.where(sub < 6, 1.0, 0.0))))
            blocks.append(block)
            tails.append(jnp.concatenate([extra, build_rhs(info[0:1], info[1:2])], axis=0).astype(BF16))
        tail = jnp.concatenate(tails, axis=1)
        block = jnp.concatenate([jnp.concatenate(blocks, axis=1), tail], axis=0)
        inner = lax.dot_general(block, weights[...], (((0,), (0,)), ((), ())), preferred_element_type=F32)
        kern = jnp.exp(inner).astype(BF16)
        tile[pl.ds(pl.multiple_of(g * group, group), group), :] = kern
        acc[...] += jnp.dot(tail, kern, preferred_element_type=F32)
        return carry

    lax.fori_loop(0, nx, first_pass, 0)

    to_cols((lambda peer: acc.at[pl.ds(RHS, RHS), pl.ds(pl.multiple_of(peer * LANES, LANES), LANES)],
             rs1.at[col], s_rs1, r_rs1))
    low_i = v_i[...].astype(BF16).astype(F32)
    s1_msg[...] = as_row((
        rowsum(v0 * v0), scale * rowsum(low_i * acc[RHS:2 * RHS, :]) + rowsum(shift * low * low)))
    to_cols((lambda peer: s1_msg, s1_col.at[col], s_s1c, r_s1c))
    wait_bytes(rs1, r_rs1)
    q1 = scale * jnp.sum(rs1[...], axis=0) + shift * low
    q1_msg[...] = q1
    to_rows((q1_msg, j2.at[row], s_q1r, r_q1r.at[x]))
    to_cols((lambda peer: q1_msg, i2.at[col], s_q1c, r_q1c))
    wait_bytes(s1_col, r_s1c)
    s1_sum[...] = jnp.sum(s1_col[...], axis=0)
    to_rows((s1_sum, s1_row.at[row], s_s1r, r_s1r))

    wait_bytes(rs1.at[pl.ds(0, nc - 1)], s_rs1)
    acc[...] = jnp.zeros_like(acc)

    def second_pass(t, carry):
        g = (x + turn(t)) % nx
        wait_bytes(j2.at[pl.ds(g * ny, ny)], r_q1r.at[g])
        value = jnp.concatenate([j2[g * ny + k] for k in range(ny)], axis=1)
        high = value.astype(BF16).astype(F32)
        both = jnp.concatenate([high, value - high], axis=0).astype(BF16)
        acc[...] += jnp.dot(both, tile[pl.ds(pl.multiple_of(g * group, group), group), :],
                            preferred_element_type=F32)
        return carry

    lax.fori_loop(0, nx, second_pass, 0)
    wait_bytes(i2, r_q1c)
    wait_bytes(s1_row, r_s1r)
    total1 = jnp.sum(s1_row[...], axis=0)
    rr0 = from_row(total1, 0)
    curve1 = from_row(total1, 1)
    alpha1 = rr0 / curve1
    r1 = v0 - alpha1 * q1

    cross = jnp.zeros((RHS, LANES), F32)
    for c in range(nc):
        part = slice(c * LANES, (c + 1) * LANES)
        second = acc[0:RHS, part] + acc[RHS:2 * RHS, part]
        out2[c] = second
        cross = cross + (v_i[:, part] - alpha1 * i2[c]) * second
    s2_msg[...] = as_row((rowsum(scale * cross + shift * r1 * q1), rowsum(r1 * r1), rowsum(r1 * q1)))
    to_cols((lambda peer: s2_msg, s2_col.at[col], s_s2c, r_s2c))
    to_cols((lambda peer: out2.at[peer], rs2.at[col], s_rs2, r_rs2))
    wait_bytes(s2_col, r_s2c)
    s2_sum[...] = jnp.sum(s2_col[...], axis=0)
    to_rows((s2_sum, s2_row.at[row], s_s2r, r_s2r))
    wait_bytes(rs2, r_rs2)
    q2 = scale * jnp.sum(rs2[...], axis=0) + shift * q1

    wait_bytes(ip.at[pl.ds(0, nc - 1)], s_pc)
    wait_bytes(jp.at[pl.ds(0, nr - 1)], s_pr)
    wait_bytes(ia.at[pl.ds(0, nc - 1)], s_ac)
    wait_bytes(ja.at[pl.ds(0, nr - 1)], s_ar)
    wait_bytes(s1_col.at[pl.ds(0, nc - 1)], s_s1c)
    wait_bytes(s1_row.at[pl.ds(0, nr - 1)], s_s1r)
    wait_bytes(j2.at[pl.ds(0, nr - 1)], s_q1r)
    wait_bytes(i2.at[pl.ds(0, nc - 1)], s_q1c)
    wait_bytes(s2_col.at[pl.ds(0, nc - 1)], s_s2c)
    wait_bytes(rs2.at[pl.ds(0, nc - 1)], s_rs2)
    wait_bytes(s2_row.at[pl.ds(0, nr - 1)], s_s2r)

    wait_bytes(s2_row, r_s2r)
    total2 = jnp.sum(s2_row[...], axis=0)
    r1q2, rr1, r1q1 = (from_row(total2, q) for q in range(3))
    beta = rr1 / rr0
    curve2 = (r1q1 - alpha1 * r1q2) + 2.0 * beta * r1q1 + beta * beta * curve1
    alpha2 = rr1 / curve2
    d2 = r1 + beta * v0
    image2 = (q1 - alpha1 * q2) + beta * q1
    sol[...] = alpha1 * v0 + alpha2 * d2
    res[...] = r1 - alpha2 * image2


def solution(mesh):
    nr, nc = mesh.shape["row"], mesh.shape["col"]
    ny = 8 if nr % 8 == 0 else nr
    nx = nr // ny
    vmem = pl.BlockSpec(memory_space=pltpu.VMEM)
    anywhere = pl.BlockSpec(memory_space=pl.ANY)
    dma = pltpu.SemaphoreType.DMA

    def shards(points, inv_scale, amplitude, noise, targets, probe_seeds):
        out = jax.ShapeDtypeStruct((RHS, LANES), F32)
        line = pltpu.VMEM((1, LANES), F32)
        plane = pltpu.VMEM((RHS, LANES), F32)
        return pl.pallas_call(
            lambda *refs: body(nx, ny, nc, refs),
            out_shape=(out, out),
            in_specs=[anywhere] * 6,
            out_specs=(vmem, vmem),
            scratch_shapes=[
                pltpu.VMEM((F, LANES), BF16), pltpu.VMEM((1, F), F32), pltpu.VMEM((1, 1), F32),
                line, line, pltpu.VMEM((1, LANES), jnp.int32),
                pltpu.VMEM((F, LANES), BF16), pltpu.VMEM((2, LANES), F32),
                pltpu.VMEM((nr, F, LANES), BF16), pltpu.VMEM((nr, 2, LANES), F32),
                pltpu.VMEM((nc, F, LANES), BF16), pltpu.VMEM((nc, 2, LANES), F32),
                pltpu.VMEM((ROWS, nc * LANES), BF16), pltpu.VMEM((RHS, nc * LANES), F32),
                pltpu.VMEM((nr * LANES, nc * LANES), BF16), pltpu.VMEM((2 * RHS, nc * LANES), F32),
                pltpu.VMEM((nc, RHS, LANES), F32), line, pltpu.VMEM((nc, 1, LANES), F32), line,
                pltpu.VMEM((nr, 1, LANES), F32),
                plane, pltpu.VMEM((nr, RHS, LANES), F32), pltpu.VMEM((nc, RHS, LANES), F32),
                pltpu.VMEM((nc, RHS, LANES), F32),
                line, pltpu.VMEM((nc, 1, LANES), F32), pltpu.VMEM((nc, RHS, LANES), F32), line,
                pltpu.VMEM((nr, 1, LANES), F32),
                dma((6,)), dma, dma, dma, dma((nx,)), dma, dma, dma, dma((nx,)), dma, dma, dma, dma, dma, dma,
                dma, dma, dma, dma((nx,)), dma, dma, dma, dma, dma, dma,
            ],
            compiler_params=pltpu.CompilerParams(
                collective_id=0, has_side_effects=True, vmem_limit_bytes=48 * 2**20),
        )(points, inv_scale.reshape(1, F), amplitude.reshape(1, 1), noise.reshape(1, LANES),
          targets.reshape(1, LANES), probe_seeds.reshape(1, LANES))

    spec = P(("row", "col"))
    both = P(None, ("row", "col"))
    return jax.shard_map(
        shards, mesh=mesh, in_specs=(both, P(), P(), spec, spec, spec),
        out_specs=(both, both), check_vma=False)
```

```python
import jax
import jax.numpy as jnp
from jax import lax
from jax.experimental import pallas as pl
from jax.experimental.pallas import tpu as pltpu
from jax.sharding import PartitionSpec as P

MESH = pl.DeviceIdType.MESH
F = 32
TAIL = 16
ROWS = F + TAIL
RHS = 8
LANES = 128
F32 = jnp.float32
BF16 = jnp.bfloat16


def pieces(value):
    first = value.astype(BF16).astype(F32)
    rest = value - first
    second = rest.astype(BF16).astype(F32)
    return first, second, rest - second


def wait_bytes(ref, sem):
    pltpu.make_async_copy(ref, ref, sem).wait()


def body(nx, ny, nc, refs):
    (points_in, inv_in, amp_in, noise_in, targets_in, seeds_in, sol, res) = refs[:8]
    (points, inv, amp, noise, targets, seeds) = refs[8:14]
    (pts, aux, jp, ja, ip, ia, weights, v_i, tile, acc, rs1, s1_msg, s1_col, s1_sum, s1_row,
     q1_msg, j2, i2, out2, s2_msg, s2_col, rs2, s2_sum, s2_row) = refs[14:38]
    (in_sem, s_pc, s_pr, s_px, r_pc, r_py, r_px, s_ac, s_ar, s_ax, r_ac, r_ay, r_ax, s_rs1, r_rs1, s_s1c, r_s1c, s_s1r, r_s1r,
     s_q1c, s_q1r, r_q1c, r_q1r, s_s2c, r_s2c, s_rs2, r_rs2, s_s2r, r_s2r) = refs[38:]
    nr = nx * ny
    group = ny * LANES
    row = lax.axis_index("row")
    col = lax.axis_index("col")
    x = row // ny
    y = row % ny

    def turn(t):
        return (t * (7 - t) // 2) % 4 if nx == 4 else t

    def row_peer(k):
        return ((x + nx - turn(k // ny)) % nx) * ny + (y + k % ny) % ny

    def col_peer(k):
        return (col + k) % nc

    def y_peer(k):
        return (x * ny + (y + k) % ny, col)

    def x_peer(k):
        return (((x + k) % nx) * ny + y, col)

    def near(t):
        half = t // 2 + 1
        return half + (t % 2) * (ny - 2 * half)

    def to_rows(*copies):
        for src, dst, send, recv in copies:
            pltpu.make_async_copy(src, dst, recv).start()

        def go(k, carry):
            peer = row_peer(k)
            for src, dst, send, recv in copies:
                pltpu.make_async_remote_copy(
                    src_ref=src, dst_ref=dst, send_sem=send, recv_sem=recv,
                    device_id=(peer, col), device_id_type=MESH,
                ).start()
            return carry

        lax.fori_loop(1, nr, go, 0)

    def to_cols(*copies):
        for src_of, dst, send, recv in copies:
            pltpu.make_async_copy(src_of(col), dst, recv).start()

        def go(k, carry):
            peer = col_peer(k)
            for src_of, dst, send, recv in copies:
                pltpu.make_async_remote_copy(
                    src_ref=src_of(peer), dst_ref=dst, send_sem=send, recv_sem=recv,
                    device_id=(row, peer), device_id_type=MESH,
                ).start()
            return carry

        lax.fori_loop(1, nc, go, 0)

    loads = [pltpu.make_async_copy(a, b, in_sem.at[n]) for n, (a, b) in enumerate((
        (points_in, points), (inv_in, inv), (targets_in, targets), (seeds_in, seeds),
        (noise_in, noise), (amp_in, amp)))]
    for load in loads:
        load.start()

    barrier = pltpu.get_barrier_semaphore()

    def greet(peer_of):
        def go(k, carry):
            pl.semaphore_signal(barrier, inc=1, device_id=peer_of(k), device_id_type=MESH)
            return carry

        return go

    lax.fori_loop(1, ny, greet(y_peer), 0)
    lax.fori_loop(1, nx, greet(x_peer), 0)
    lax.fori_loop(1, nc, greet(lambda k: (row, col_peer(k))), 0)

    sub = lax.broadcasted_iota(jnp.int32, (RHS, LANES), 0)
    lane = lax.broadcasted_iota(jnp.int32, (RHS, LANES), 1)

    def build_rhs(target, seed):
        bits = (seed.astype(jnp.int32) >> jnp.maximum(sub - 1, 0)) & 1
        return jnp.where(sub == 0, target, (1 - 2 * bits).astype(F32))

    def minus_half_norm(block):
        values = block.astype(F32)
        return -0.5 * jnp.sum(values * values, axis=0, keepdims=True)

    def as_row(sums):
        spread = jnp.zeros((RHS, LANES), F32)
        for q, value in enumerate(sums):
            spread = spread + jnp.where(lane == q * RHS + sub, value, 0.0)
        return jnp.sum(spread, axis=0, keepdims=True)

    def from_row(total, q):
        return jnp.sum(jnp.where(lane == q * RHS + sub, total, 0.0), axis=1, keepdims=True)

    def rowsum(value):
        return jnp.sum(value, axis=1, keepdims=True)

    for load in loads:
        load.wait()
    eye = lax.broadcasted_iota(jnp.int32, (F, F), 0) == lax.broadcasted_iota(jnp.int32, (F, F), 1)
    factor = jnp.sum(jnp.where(eye, inv[...], 0.0), axis=1, keepdims=True)
    pts[...] = (points[...].astype(F32) * factor).astype(BF16)
    aux[0:1, :] = targets[...]
    aux[1:2, :] = seeds[...].astype(F32)

    pl.semaphore_wait(barrier, ny - 1 + nx - 1 + nc - 1)
    to_cols((lambda peer: aux, ia.at[col], s_ac, r_ac), (lambda peer: pts, ip.at[col], s_pc, r_pc))

    def copy_to(device, src, dst, send, recv):
        pltpu.make_async_remote_copy(
            src_ref=src, dst_ref=dst, send_sem=send, recv_sem=recv,
            device_id=device, device_id_type=MESH,
        ).start()

    def forward(slot):
        def go(k, carry):
            copy_to(x_peer(k), ja.at[slot], ja.at[slot], s_ax, r_ax.at[x])
            copy_to(x_peer(k), jp.at[slot], jp.at[slot], s_px, r_px.at[x])
            return carry

        lax.fori_loop(1, nx, go, 0)

    def to_ring(t, carry):
        peer = y_peer(near(ny - 2 - t))
        copy_to(peer, aux, ja.at[row], s_ar, r_ay.at[y])
        copy_to(peer, pts, jp.at[row], s_pr, r_py.at[y])
        return carry

    lax.fori_loop(0, ny - 1, to_ring, 0)
    ja[row] = aux[...]
    jp[row] = pts[...]
    forward(row)

    def pass_on(t, carry):
        source = (y + near(t)) % ny
        slot = x * ny + source
        wait_bytes(ja.at[slot], r_ay.at[source])
        wait_bytes(jp.at[slot], r_py.at[source])
        forward(slot)
        return carry

    lax.fori_loop(0, ny - 1, pass_on, 0)
    v0 = build_rhs(targets[...], seeds[...])
    low = v0.astype(BF16).astype(F32)
    scale = amp[...]
    shift = noise[...]
    acc[...] = jnp.zeros_like(acc)

    wait_bytes(ia, r_ac)
    wait_bytes(ip, r_pc)
    for c in range(nc):
        part = slice(c * LANES, (c + 1) * LANES)
        block = ip[c]
        n1, n2, n3 = pieces(minus_half_norm(block))
        weights[0:F, part] = block
        extra = jnp.where(sub < 3, 1.0, jnp.where(sub == 3, n1, jnp.where(sub == 4, n2, jnp.where(sub == 5, n3, 0.0))))
        weights[F:ROWS, part] = jnp.concatenate([extra, jnp.zeros_like(extra)], axis=0).astype(BF16)
        v_i[:, part] = build_rhs(ia[c, 0:1], ia[c, 1:2])

    def first_pass(t, carry):
        g = (x + turn(t)) % nx

        @pl.when(t > 0)
        def _():
            wait_bytes(ja.at[pl.ds(g * ny, ny)], r_ax.at[g])
            wait_bytes(jp.at[pl.ds(g * ny, ny)], r_px.at[g])

        blocks, tails = [], []
        for k in range(ny):
            block = jp[g * ny + k]
            info = ja[g * ny + k]
            n1, n2, n3 = pieces(minus_half_norm(block))
            extra = jnp.where(sub == 0, n1, jnp.where(sub == 1, n2, jnp.where(sub == 2, n3, jnp.where(sub < 6, 1.0, 0.0))))
            blocks.append(block)
            tails.append(jnp.concatenate([extra, build_rhs(info[0:1], info[1:2])], axis=0).astype(BF16))
        tail = jnp.concatenate(tails, axis=1)
        block = jnp.concatenate([jnp.concatenate(blocks, axis=1), tail], axis=0)
        inner = lax.dot_general(block, weights[...], (((0,), (0,)), ((), ())), preferred_element_type=F32)
        kern = jnp.exp(inner).astype(BF16)
        tile[pl.ds(pl.multiple_of(g * group, group), group), :] = kern
        acc[...] += jnp.dot(tail, kern, preferred_element_type=F32)
        return carry

    lax.fori_loop(0, nx, first_pass, 0)

    to_cols((lambda peer: acc.at[pl.ds(RHS, RHS), pl.ds(pl.multiple_of(peer * LANES, LANES), LANES)],
             rs1.at[col], s_rs1, r_rs1))
    low_i = v_i[...].astype(BF16).astype(F32)
    s1_msg[...] = as_row((
        rowsum(v0 * v0), scale * rowsum(low_i * acc[RHS:2 * RHS, :]) + rowsum(shift * low * low)))
    to_cols((lambda peer: s1_msg, s1_col.at[col], s_s1c, r_s1c))
    wait_bytes(rs1, r_rs1)
    q1 = scale * jnp.sum(rs1[...], axis=0) + shift * low
    q1_msg[...] = q1
    to_rows((q1_msg, j2.at[row], s_q1r, r_q1r.at[x]))
    wait_bytes(s1_col, r_s1c)
    s1_sum[...] = jnp.sum(s1_col[...], axis=0)
    to_rows((s1_sum, s1_row.at[row], s_s1r, r_s1r))
    to_cols((lambda peer: q1_msg, i2.at[col], s_q1c, r_q1c))

    wait_bytes(rs1.at[pl.ds(0, nc - 1)], s_rs1)
    acc[...] = jnp.zeros_like(acc)

    def second_pass(t, carry):
        g = (x + turn(t)) % nx
        wait_bytes(j2.at[pl.ds(g * ny, ny)], r_q1r.at[g])
        value = jnp.concatenate([j2[g * ny + k] for k in range(ny)], axis=1)
        high = value.astype(BF16).astype(F32)
        both = jnp.concatenate([high, value - high], axis=0).astype(BF16)
        acc[...] += jnp.dot(both, tile[pl.ds(pl.multiple_of(g * group, group), group), :],
                            preferred_element_type=F32)
        return carry

    lax.fori_loop(0, nx, second_pass, 0)
    wait_bytes(i2, r_q1c)
    wait_bytes(s1_row, r_s1r)
    total1 = jnp.sum(s1_row[...], axis=0)
    rr0 = from_row(total1, 0)
    curve1 = from_row(total1, 1)
    alpha1 = rr0 / curve1
    r1 = v0 - alpha1 * q1

    cross = jnp.zeros((RHS, LANES), F32)
    for c in range(nc):
        part = slice(c * LANES, (c + 1) * LANES)
        second = acc[0:RHS, part] + acc[RHS:2 * RHS, part]
        out2[c] = second
        cross = cross + (v_i[:, part] - alpha1 * i2[c]) * second
    s2_msg[...] = as_row((rowsum(scale * cross + shift * r1 * q1), rowsum(r1 * r1), rowsum(r1 * q1)))
    to_cols((lambda peer: s2_msg, s2_col.at[col], s_s2c, r_s2c))
    to_cols((lambda peer: out2.at[peer], rs2.at[col], s_rs2, r_rs2))
    wait_bytes(s2_col, r_s2c)
    s2_sum[...] = jnp.sum(s2_col[...], axis=0)
    to_rows((s2_sum, s2_row.at[row], s_s2r, r_s2r))
    wait_bytes(rs2, r_rs2)
    q2 = scale * jnp.sum(rs2[...], axis=0) + shift * q1

    wait_bytes(ip.at[pl.ds(0, nc - 1)], s_pc)
    wait_bytes(jp.at[pl.ds(0, ny - 1)], s_pr)
    wait_bytes(jp.at[pl.ds(0, nr - ny)], s_px)
    wait_bytes(ia.at[pl.ds(0, nc - 1)], s_ac)
    wait_bytes(ja.at[pl.ds(0, ny - 1)], s_ar)
    wait_bytes(ja.at[pl.ds(0, nr - ny)], s_ax)
    wait_bytes(s1_col.at[pl.ds(0, nc - 1)], s_s1c)
    wait_bytes(s1_row.at[pl.ds(0, nr - 1)], s_s1r)
    wait_bytes(j2.at[pl.ds(0, nr - 1)], s_q1r)
    wait_bytes(i2.at[pl.ds(0, nc - 1)], s_q1c)
    wait_bytes(s2_col.at[pl.ds(0, nc - 1)], s_s2c)
    wait_bytes(rs2.at[pl.ds(0, nc - 1)], s_rs2)
    wait_bytes(s2_row.at[pl.ds(0, nr - 1)], s_s2r)

    wait_bytes(s2_row, r_s2r)
    total2 = jnp.sum(s2_row[...], axis=0)
    r1q2, rr1, r1q1 = (from_row(total2, q) for q in range(3))
    beta = rr1 / rr0
    curve2 = (r1q1 - alpha1 * r1q2) + 2.0 * beta * r1q1 + beta * beta * curve1
    alpha2 = rr1 / curve2
    d2 = r1 + beta * v0
    image2 = (q1 - alpha1 * q2) + beta * q1
    sol[...] = alpha1 * v0 + alpha2 * d2
    res[...] = r1 - alpha2 * image2


def solution(mesh):
    nr, nc = mesh.shape["row"], mesh.shape["col"]
    ny = 8 if nr % 8 == 0 else nr
    nx = nr // ny
    vmem = pl.BlockSpec(memory_space=pltpu.VMEM)
    anywhere = pl.BlockSpec(memory_space=pl.ANY)
    dma = pltpu.SemaphoreType.DMA

    def shards(points, inv_scale, amplitude, noise, targets, probe_seeds):
        out = jax.ShapeDtypeStruct((RHS, LANES), F32)
        line = pltpu.VMEM((1, LANES), F32)
        plane = pltpu.VMEM((RHS, LANES), F32)
        return pl.pallas_call(
            lambda *refs: body(nx, ny, nc, refs),
            out_shape=(out, out),
            in_specs=[anywhere] * 6,
            out_specs=(vmem, vmem),
            scratch_shapes=[
                pltpu.VMEM((F, LANES), BF16), pltpu.VMEM((1, F), F32), pltpu.VMEM((1, 1), F32),
                line, line, pltpu.VMEM((1, LANES), jnp.int32),
                pltpu.VMEM((F, LANES), BF16), pltpu.VMEM((2, LANES), F32),
                pltpu.VMEM((nr, F, LANES), BF16), pltpu.VMEM((nr, 2, LANES), F32),
                pltpu.VMEM((nc, F, LANES), BF16), pltpu.VMEM((nc, 2, LANES), F32),
                pltpu.VMEM((ROWS, nc * LANES), BF16), pltpu.VMEM((RHS, nc * LANES), F32),
                pltpu.VMEM((nr * LANES, nc * LANES), BF16), pltpu.VMEM((2 * RHS, nc * LANES), F32),
                pltpu.VMEM((nc, RHS, LANES), F32), line, pltpu.VMEM((nc, 1, LANES), F32), line,
                pltpu.VMEM((nr, 1, LANES), F32),
                plane, pltpu.VMEM((nr, RHS, LANES), F32), pltpu.VMEM((nc, RHS, LANES), F32),
                pltpu.VMEM((nc, RHS, LANES), F32),
                line, pltpu.VMEM((nc, 1, LANES), F32), pltpu.VMEM((nc, RHS, LANES), F32), line,
                pltpu.VMEM((nr, 1, LANES), F32),
                dma((6,)), dma, dma, dma, dma, dma((ny,)), dma((nx,)), dma, dma, dma, dma, dma((ny,)), dma((nx,)), dma, dma, dma, dma, dma, dma,
                dma, dma, dma, dma((nx,)), dma, dma, dma, dma, dma, dma,
            ],
            compiler_params=pltpu.CompilerParams(
                collective_id=0, has_side_effects=True, vmem_limit_bytes=48 * 2**20),
        )(points, inv_scale.reshape(1, F), amplitude.reshape(1, 1), noise.reshape(1, LANES),
          targets.reshape(1, LANES), probe_seeds.reshape(1, LANES))

    spec = P(("row", "col"))
    both = P(None, ("row", "col"))
    return jax.shard_map(
        shards, mesh=mesh, in_specs=(both, P(), P(), spec, spec, spec),
        out_specs=(both, both), check_vma=False)
```

```python
import jax
import jax.numpy as jnp
from jax import lax
from jax.experimental import pallas as pl
from jax.experimental.pallas import tpu as pltpu
from jax.sharding import PartitionSpec as P

MESH = pl.DeviceIdType.MESH
F = 32
TAIL = 16
ROWS = F + TAIL
RHS = 8
LANES = 128
F32 = jnp.float32
BF16 = jnp.bfloat16


def pieces(value):
    first = value.astype(BF16).astype(F32)
    rest = value - first
    second = rest.astype(BF16).astype(F32)
    return first, second, rest - second


def wait_bytes(ref, sem):
    pltpu.make_async_copy(ref, ref, sem).wait()


def body(nx, ny, nc, refs):
    (points_in, inv_in, amp_in, noise_in, targets_in, seeds_in, both) = refs[:7]
    (points, inv, amp, noise, targets, seeds) = refs[7:13]
    (pts, aux, jp, ja, ip, ia, weights, v_i, tile, acc, rs1, s1_msg, s1_col, s1_sum, s1_row,
     q1_msg, j2, i2, out2, s2_msg, s2_col, rs2, s2_sum, s2_row) = refs[13:37]
    (in_sem, s_pc, s_pr, s_px, r_pc, r_py, r_px, s_ac, s_ar, s_ax, r_ac, r_ay, r_ax, s_rs1, r_rs1, s_s1c, r_s1c, s_s1r, r_s1r,
     s_q1c, s_q1r, r_q1c, r_q1r, s_s2c, r_s2c, s_rs2, r_rs2, s_s2r, r_s2r) = refs[37:]
    nr = nx * ny
    group = ny * LANES
    row = lax.axis_index("row")
    col = lax.axis_index("col")
    x = row // ny
    y = row % ny
    nz = nc // 2
    z = col // 2
    core = col % 2

    def turn(t):
        return (t * (7 - t) // 2) % 4 if nx == 4 else t

    def offset(t, n):
        half = (t + 1) // 2
        return (t % 2) * half + (1 - t % 2) * ((n - half) % n)

    def row_peer(k):
        far_y, far_x = ny - 1 - k // nx, nx - 1 - k % nx
        return ((x + offset(far_x, nx)) % nx) * ny + (y + offset(far_y, ny)) % ny

    def col_peer(k):
        far_z, far_core = nz - 1 - k // 2, 1 - k % 2
        return ((z + offset(far_z, nz)) % nz) * 2 + (core + far_core) % 2

    def y_peer(k):
        return (x * ny + (y + k) % ny, col)

    def x_peer(k):
        return (((x + k) % nx) * ny + y, col)

    def near(t):
        half = t // 2 + 1
        return half + (t % 2) * (ny - 2 * half)

    def to_rows(*copies):
        for src, dst, send, recv in copies:
            pltpu.make_async_copy(src, dst, recv).start()

        def go(k, carry):
            peer = row_peer(k)
            for src, dst, send, recv in copies:
                pltpu.make_async_remote_copy(
                    src_ref=src, dst_ref=dst, send_sem=send, recv_sem=recv,
                    device_id=(peer, col), device_id_type=MESH,
                ).start()
            return carry

        lax.fori_loop(0, nr - 1, go, 0)

    def to_cols(*copies):
        for src_of, dst, send, recv in copies:
            pltpu.make_async_copy(src_of(col), dst, recv).start()

        def go(k, carry):
            peer = col_peer(k)
            for src_of, dst, send, recv in copies:
                pltpu.make_async_remote_copy(
                    src_ref=src_of(peer), dst_ref=dst, send_sem=send, recv_sem=recv,
                    device_id=(row, peer), device_id_type=MESH,
                ).start()
            return carry

        lax.fori_loop(0, nc - 1, go, 0)

    loads = [pltpu.make_async_copy(a, b, in_sem.at[n]) for n, (a, b) in enumerate((
        (points_in, points), (inv_in, inv), (targets_in, targets), (seeds_in, seeds),
        (noise_in, noise), (amp_in, amp)))]
    for load in loads:
        load.start()

    barrier = pltpu.get_barrier_semaphore()

    def greet(peer_of):
        def go(k, carry):
            pl.semaphore_signal(barrier, inc=1, device_id=peer_of(k), device_id_type=MESH)
            return carry

        return go

    lax.fori_loop(1, ny, greet(y_peer), 0)
    lax.fori_loop(1, nx, greet(x_peer), 0)
    lax.fori_loop(0, nc - 1, greet(lambda k: (row, col_peer(k))), 0)

    sub = lax.broadcasted_iota(jnp.int32, (RHS, LANES), 0)
    lane = lax.broadcasted_iota(jnp.int32, (RHS, LANES), 1)

    def build_rhs(target, seed):
        bits = (seed.astype(jnp.int32) >> jnp.maximum(sub - 1, 0)) & 1
        return jnp.where(sub == 0, target, (1 - 2 * bits).astype(F32))

    def minus_half_norm(block):
        values = block.astype(F32)
        return -0.5 * jnp.sum(values * values, axis=0, keepdims=True)

    def as_row(sums):
        spread = jnp.zeros((RHS, LANES), F32)
        for q, value in enumerate(sums):
            spread = spread + jnp.where(lane == q * RHS + sub, value, 0.0)
        return jnp.sum(spread, axis=0, keepdims=True)

    def from_row(total, q):
        return jnp.sum(jnp.where(lane == q * RHS + sub, total, 0.0), axis=1, keepdims=True)

    def rowsum(value):
        return jnp.sum(value, axis=1, keepdims=True)

    for load in loads:
        load.wait()
    eye = lax.broadcasted_iota(jnp.int32, (F, F), 0) == lax.broadcasted_iota(jnp.int32, (F, F), 1)
    factor = jnp.sum(jnp.where(eye, inv[...], 0.0), axis=1, keepdims=True)
    pts[...] = (points[...].astype(F32) * factor).astype(BF16)
    aux[0:1, :] = targets[...]
    aux[1:2, :] = seeds[...].astype(F32)

    pl.semaphore_wait(barrier, ny - 1 + nx - 1 + nc - 1)
    to_cols((lambda peer: aux, ia.at[col], s_ac, r_ac), (lambda peer: pts, ip.at[col], s_pc, r_pc))

    def copy_to(device, src, dst, send, recv):
        pltpu.make_async_remote_copy(
            src_ref=src, dst_ref=dst, send_sem=send, recv_sem=recv,
            device_id=device, device_id_type=MESH,
        ).start()

    def forward(slot):
        def go(k, carry):
            copy_to(x_peer(k), ja.at[slot], ja.at[slot], s_ax, r_ax.at[x])
            copy_to(x_peer(k), jp.at[slot], jp.at[slot], s_px, r_px.at[x])
            return carry

        lax.fori_loop(1, nx, go, 0)

    def to_ring(t, carry):
        peer = y_peer(near(ny - 2 - t))
        copy_to(peer, aux, ja.at[row], s_ar, r_ay.at[y])
        copy_to(peer, pts, jp.at[row], s_pr, r_py.at[y])
        return carry

    lax.fori_loop(0, ny - 1, to_ring, 0)
    ja[row] = aux[...]
    jp[row] = pts[...]
    forward(row)

    def pass_on(t, carry):
        source = (y + near(t)) % ny
        slot = x * ny + source
        wait_bytes(ja.at[slot], r_ay.at[source])
        wait_bytes(jp.at[slot], r_py.at[source])
        forward(slot)
        return carry

    lax.fori_loop(0, ny - 1, pass_on, 0)
    v0 = build_rhs(targets[...], seeds[...])
    low = v0.astype(BF16).astype(F32)
    scale = amp[...]
    shift = noise[...]
    acc[...] = jnp.zeros_like(acc)

    wait_bytes(ia, r_ac)
    wait_bytes(ip, r_pc)
    for c in range(nc):
        part = slice(c * LANES, (c + 1) * LANES)
        block = ip[c]
        n1, n2, n3 = pieces(minus_half_norm(block))
        weights[0:F, part] = block
        extra = jnp.where(sub < 3, 1.0, jnp.where(sub == 3, n1, jnp.where(sub == 4, n2, jnp.where(sub == 5, n3, 0.0))))
        weights[F:ROWS, part] = jnp.concatenate([extra, jnp.zeros_like(extra)], axis=0).astype(BF16)
        v_i[:, part] = build_rhs(ia[c, 0:1], ia[c, 1:2])

    def first_pass(t, carry):
        g = (x + turn(t)) % nx

        @pl.when(t > 0)
        def _():
            wait_bytes(ja.at[pl.ds(g * ny, ny)], r_ax.at[g])
            wait_bytes(jp.at[pl.ds(g * ny, ny)], r_px.at[g])

        blocks, tails = [], []
        for k in range(ny):
            block = jp[g * ny + k]
            info = ja[g * ny + k]
            n1, n2, n3 = pieces(minus_half_norm(block))
            extra = jnp.where(sub == 0, n1, jnp.where(sub == 1, n2, jnp.where(sub == 2, n3, jnp.where(sub < 6, 1.0, 0.0))))
            blocks.append(block)
            tails.append(jnp.concatenate([extra, build_rhs(info[0:1], info[1:2])], axis=0).astype(BF16))
        tail = jnp.concatenate(tails, axis=1)
        block = jnp.concatenate([jnp.concatenate(blocks, axis=1), tail], axis=0)
        inner = lax.dot_general(block, weights[...], (((0,), (0,)), ((), ())), preferred_element_type=F32)
        kern = jnp.exp(inner).astype(BF16)
        tile[pl.ds(pl.multiple_of(g * group, group), group), :] = kern
        acc[...] += jnp.dot(tail, kern, preferred_element_type=F32)
        return carry

    lax.fori_loop(0, nx, first_pass, 0)

    to_cols((lambda peer: acc.at[pl.ds(RHS, RHS), pl.ds(pl.multiple_of(peer * LANES, LANES), LANES)],
             rs1.at[col], s_rs1, r_rs1))
    low_i = v_i[...].astype(BF16).astype(F32)
    s1_msg[...] = as_row((
        rowsum(v0 * v0), scale * rowsum(low_i * acc[RHS:2 * RHS, :]) + rowsum(shift * low * low)))
    to_cols((lambda peer: s1_msg, s1_col.at[col], s_s1c, r_s1c))
    wait_bytes(rs1, r_rs1)
    q1 = scale * jnp.sum(rs1[...], axis=0) + shift * low
    q1_msg[...] = q1
    to_rows((q1_msg, j2.at[row], s_q1r, r_q1r.at[x]))
    wait_bytes(s1_col, r_s1c)
    s1_sum[...] = jnp.sum(s1_col[...], axis=0)
    to_rows((s1_sum, s1_row.at[row], s_s1r, r_s1r))
    to_cols((lambda peer: q1_msg, i2.at[col], s_q1c, r_q1c))

    wait_bytes(rs1.at[pl.ds(0, nc - 1)], s_rs1)
    acc[...] = jnp.zeros_like(acc)

    def second_pass(t, carry):
        g = (x + turn(t)) % nx
        wait_bytes(j2.at[pl.ds(g * ny, ny)], r_q1r.at[g])
        value = jnp.concatenate([j2[g * ny + k] for k in range(ny)], axis=1)
        high = value.astype(BF16).astype(F32)
        both = jnp.concatenate([high, value - high], axis=0).astype(BF16)
        acc[...] += jnp.dot(both, tile[pl.ds(pl.multiple_of(g * group, group), group), :],
                            preferred_element_type=F32)
        return carry

    lax.fori_loop(0, nx, second_pass, 0)
    wait_bytes(i2, r_q1c)
    wait_bytes(s1_row, r_s1r)
    total1 = jnp.sum(s1_row[...], axis=0)
    rr0 = from_row(total1, 0)
    curve1 = from_row(total1, 1)
    alpha1 = rr0 / curve1
    r1 = v0 - alpha1 * q1

    cross = jnp.zeros((RHS, LANES), F32)
    for c in range(nc):
        part = slice(c * LANES, (c + 1) * LANES)
        second = acc[0:RHS, part] + acc[RHS:2 * RHS, part]
        out2[c] = second
        cross = cross + (v_i[:, part] - alpha1 * i2[c]) * second
    s2_msg[...] = as_row((rowsum(scale * cross + shift * r1 * q1), rowsum(r1 * r1), rowsum(r1 * q1)))
    to_cols((lambda peer: s2_msg, s2_col.at[col], s_s2c, r_s2c))
    to_cols((lambda peer: out2.at[peer], rs2.at[col], s_rs2, r_rs2))
    wait_bytes(s2_col, r_s2c)
    s2_sum[...] = jnp.sum(s2_col[...], axis=0)
    to_rows((s2_sum, s2_row.at[row], s_s2r, r_s2r))
    wait_bytes(rs2, r_rs2)
    q2 = scale * jnp.sum(rs2[...], axis=0) + shift * q1

    wait_bytes(ip.at[pl.ds(0, nc - 1)], s_pc)
    wait_bytes(jp.at[pl.ds(0, ny - 1)], s_pr)
    wait_bytes(jp.at[pl.ds(0, nr - ny)], s_px)
    wait_bytes(ia.at[pl.ds(0, nc - 1)], s_ac)
    wait_bytes(ja.at[pl.ds(0, ny - 1)], s_ar)
    wait_bytes(ja.at[pl.ds(0, nr - ny)], s_ax)
    wait_bytes(s1_col.at[pl.ds(0, nc - 1)], s_s1c)
    wait_bytes(s1_row.at[pl.ds(0, nr - 1)], s_s1r)
    wait_bytes(j2.at[pl.ds(0, nr - 1)], s_q1r)
    wait_bytes(i2.at[pl.ds(0, nc - 1)], s_q1c)
    wait_bytes(s2_col.at[pl.ds(0, nc - 1)], s_s2c)
    wait_bytes(rs2.at[pl.ds(0, nc - 1)], s_rs2)
    wait_bytes(s2_row.at[pl.ds(0, nr - 1)], s_s2r)

    wait_bytes(s2_row, r_s2r)
    total2 = jnp.sum(s2_row[...], axis=0)
    r1q2, rr1, r1q1 = (from_row(total2, q) for q in range(3))
    beta = rr1 / rr0
    curve2 = (r1q1 - alpha1 * r1q2) + 2.0 * beta * r1q1 + beta * beta * curve1
    alpha2 = rr1 / curve2
    d2 = r1 + beta * v0
    image2 = (q1 - alpha1 * q2) + beta * q1
    both[0] = alpha1 * v0 + alpha2 * d2
    both[1] = r1 - alpha2 * image2


def solution(mesh):
    nr, nc = mesh.shape["row"], mesh.shape["col"]
    ny = 8 if nr % 8 == 0 else nr
    nx = nr // ny
    vmem = pl.BlockSpec(memory_space=pltpu.VMEM)
    anywhere = pl.BlockSpec(memory_space=pl.ANY)
    dma = pltpu.SemaphoreType.DMA

    def shards(points, inv_scale, amplitude, noise, targets, probe_seeds):
        out = jax.ShapeDtypeStruct((2, RHS, LANES), F32)
        line = pltpu.VMEM((1, LANES), F32)
        plane = pltpu.VMEM((RHS, LANES), F32)
        pair = pl.pallas_call(
            lambda *refs: body(nx, ny, nc, refs),
            out_shape=out,
            in_specs=[anywhere] * 6,
            out_specs=vmem,
            scratch_shapes=[
                pltpu.VMEM((F, LANES), BF16), pltpu.VMEM((1, F), F32), pltpu.VMEM((1, 1), F32),
                line, line, pltpu.VMEM((1, LANES), jnp.int32),
                pltpu.VMEM((F, LANES), BF16), pltpu.VMEM((2, LANES), F32),
                pltpu.VMEM((nr, F, LANES), BF16), pltpu.VMEM((nr, 2, LANES), F32),
                pltpu.VMEM((nc, F, LANES), BF16), pltpu.VMEM((nc, 2, LANES), F32),
                pltpu.VMEM((ROWS, nc * LANES), BF16), pltpu.VMEM((RHS, nc * LANES), F32),
                pltpu.VMEM((nr * LANES, nc * LANES), BF16), pltpu.VMEM((2 * RHS, nc * LANES), F32),
                pltpu.VMEM((nc, RHS, LANES), F32), line, pltpu.VMEM((nc, 1, LANES), F32), line,
                pltpu.VMEM((nr, 1, LANES), F32),
                plane, pltpu.VMEM((nr, RHS, LANES), F32), pltpu.VMEM((nc, RHS, LANES), F32),
                pltpu.VMEM((nc, RHS, LANES), F32),
                line, pltpu.VMEM((nc, 1, LANES), F32), pltpu.VMEM((nc, RHS, LANES), F32), line,
                pltpu.VMEM((nr, 1, LANES), F32),
                dma((6,)), dma, dma, dma, dma, dma((ny,)), dma((nx,)), dma, dma, dma, dma, dma((ny,)), dma((nx,)), dma, dma, dma, dma, dma, dma,
                dma, dma, dma, dma((nx,)), dma, dma, dma, dma, dma, dma,
            ],
            compiler_params=pltpu.CompilerParams(
                collective_id=0, has_side_effects=True, vmem_limit_bytes=48 * 2**20),
        )(points, inv_scale.reshape(1, F), amplitude.reshape(1, 1), noise.reshape(1, LANES),
          targets.reshape(1, LANES), probe_seeds.reshape(1, LANES))
        return pair[0], pair[1]

    spec = P(("row", "col"))
    both = P(None, ("row", "col"))
    return jax.shard_map(
        shards, mesh=mesh, in_specs=(both, P(), P(), spec, spec, spec),
        out_specs=(both, both), check_vma=False)
```

```python
import jax
import jax.numpy as jnp
from jax import lax
from jax.experimental import pallas as pl
from jax.experimental.pallas import tpu as pltpu
from jax.sharding import PartitionSpec as P

MESH = pl.DeviceIdType.MESH
F = 32
TAIL = 16
ROWS = F + TAIL
RHS = 8
LANES = 128
F32 = jnp.float32
BF16 = jnp.bfloat16


def pieces(value):
    first = value.astype(BF16).astype(F32)
    rest = value - first
    second = rest.astype(BF16).astype(F32)
    return first, second, rest - second


def wait_bytes(ref, sem):
    pltpu.make_async_copy(ref, ref, sem).wait()


def body(nx, ny, nc, refs):
    (points_in, inv_in, amp_in, noise_in, targets_in, seeds_in, both) = refs[:7]
    (points, inv, amp, noise, targets, seeds) = refs[7:13]
    (pts, aux, jp, ja, ip, ia, weights, v_i, tile, acc, rs1, s1_msg, s1_col, s1_sum, s1_row,
     q1_msg, j2, i2, out2, s2_msg, s2_col, rs2, s2_sum, s2_row) = refs[13:37]
    (in_sem, s_pc, s_pr, s_px, r_pc, r_py, r_px, s_ac, s_ar, s_ax, r_ac, r_ay, r_ax, s_rs1, r_rs1, s_s1c, r_s1c, s_s1r, r_s1r,
     s_q1c, s_q1r, r_q1c, r_q1r, s_s2c, r_s2c, s_rs2, r_rs2, s_s2r, r_s2r) = refs[37:]
    nr = nx * ny
    group = ny * LANES
    row = lax.axis_index("row")
    col = lax.axis_index("col")
    x = row // ny
    y = row % ny
    nz = nc // 2
    z = col // 2
    core = col % 2

    def turn(t):
        return (t * (7 - t) // 2) % 4 if nx == 4 else t

    def offset(t, n):
        half = (t + 1) // 2
        return (t % 2) * half + (1 - t % 2) * ((n - half) % n)

    def row_peer(k):
        far_y, far_x = ny - 1 - k // nx, nx - 1 - k % nx
        return ((x + offset(far_x, nx)) % nx) * ny + (y + offset(far_y, ny)) % ny

    def col_peer(k):
        far_z, far_core = nz - 1 - k // 2, 1 - k % 2
        return ((z + offset(far_z, nz)) % nz) * 2 + (core + far_core) % 2

    def row_peer_x(k):
        far_x, far_y = nx - 1 - k // ny, ny - 1 - k % ny
        return ((x + offset(far_x, nx)) % nx) * ny + (y + offset(far_y, ny)) % ny

    def row_peer_n(k):
        near_x, near_y = (k + 1) // ny, (k + 1) % ny
        return ((x + nx - turn(near_x)) % nx) * ny + (y + near_y) % ny

    def y_peer(k):
        return (x * ny + (y + k) % ny, col)

    def x_peer(k):
        return (((x + k) % nx) * ny + y, col)

    def near(t):
        half = t // 2 + 1
        return half + (t % 2) * (ny - 2 * half)

    def to_rows(*copies, peer_of=row_peer):
        for src, dst, send, recv in copies:
            pltpu.make_async_copy(src, dst, recv).start()

        def go(k, carry):
            peer = peer_of(k)
            for src, dst, send, recv in copies:
                pltpu.make_async_remote_copy(
                    src_ref=src, dst_ref=dst, send_sem=send, recv_sem=recv,
                    device_id=(peer, col), device_id_type=MESH,
                ).start()
            return carry

        lax.fori_loop(0, nr - 1, go, 0)

    def to_cols(*copies):
        for src_of, dst, send, recv in copies:
            pltpu.make_async_copy(src_of(col), dst, recv).start()

        def go(k, carry):
            peer = col_peer(k)
            for src_of, dst, send, recv in copies:
                pltpu.make_async_remote_copy(
                    src_ref=src_of(peer), dst_ref=dst, send_sem=send, recv_sem=recv,
                    device_id=(row, peer), device_id_type=MESH,
                ).start()
            return carry

        lax.fori_loop(0, nc - 1, go, 0)

    loads = [pltpu.make_async_copy(a, b, in_sem.at[n]) for n, (a, b) in enumerate((
        (points_in, points), (inv_in, inv), (targets_in, targets), (seeds_in, seeds),
        (noise_in, noise), (amp_in, amp)))]
    for load in loads:
        load.start()

    barrier = pltpu.get_barrier_semaphore()

    def greet(peer_of):
        def go(k, carry):
            pl.semaphore_signal(barrier, inc=1, device_id=peer_of(k), device_id_type=MESH)
            return carry

        return go

    lax.fori_loop(1, ny, greet(y_peer), 0)
    lax.fori_loop(1, nx, greet(x_peer), 0)
    lax.fori_loop(0, nc - 1, greet(lambda k: (row, col_peer(k))), 0)

    sub = lax.broadcasted_iota(jnp.int32, (RHS, LANES), 0)
    lane = lax.broadcasted_iota(jnp.int32, (RHS, LANES), 1)

    def build_rhs(target, seed):
        bits = (seed.astype(jnp.int32) >> jnp.maximum(sub - 1, 0)) & 1
        return jnp.where(sub == 0, target, (1 - 2 * bits).astype(F32))

    def minus_half_norm(block):
        values = block.astype(F32)
        return -0.5 * jnp.sum(values * values, axis=0, keepdims=True)

    def as_row(sums):
        spread = jnp.zeros((RHS, LANES), F32)
        for q, value in enumerate(sums):
            spread = spread + jnp.where(lane == q * RHS + sub, value, 0.0)
        return jnp.sum(spread, axis=0, keepdims=True)

    def from_row(total, q):
        return jnp.sum(jnp.where(lane == q * RHS + sub, total, 0.0), axis=1, keepdims=True)

    def rowsum(value):
        return jnp.sum(value, axis=1, keepdims=True)

    for load in loads:
        load.wait()
    eye = lax.broadcasted_iota(jnp.int32, (F, F), 0) == lax.broadcasted_iota(jnp.int32, (F, F), 1)
    factor = jnp.sum(jnp.where(eye, inv[...], 0.0), axis=1, keepdims=True)
    pts[...] = (points[...].astype(F32) * factor).astype(BF16)
    aux[0:1, :] = targets[...]
    aux[1:2, :] = seeds[...].astype(F32)

    pl.semaphore_wait(barrier, ny - 1 + nx - 1 + nc - 1)
    to_cols((lambda peer: pts, ip.at[col], s_pc, r_pc))

    def copy_to(device, src, dst, send, recv):
        pltpu.make_async_remote_copy(
            src_ref=src, dst_ref=dst, send_sem=send, recv_sem=recv,
            device_id=device, device_id_type=MESH,
        ).start()

    def forward(slot):
        def go(k, carry):
            copy_to(x_peer(k), ja.at[slot], ja.at[slot], s_ax, r_ax.at[x])
            copy_to(x_peer(k), jp.at[slot], jp.at[slot], s_px, r_px.at[x])
            return carry

        lax.fori_loop(1, nx, go, 0)

    def to_ring(t, carry):
        peer = y_peer(near(ny - 2 - t))
        copy_to(peer, aux, ja.at[row], s_ar, r_ay.at[y])
        copy_to(peer, pts, jp.at[row], s_pr, r_py.at[y])
        return carry

    lax.fori_loop(0, ny - 1, to_ring, 0)
    ja[row] = aux[...]
    jp[row] = pts[...]
    forward(row)
    to_cols((lambda peer: aux, ia.at[col], s_ac, r_ac))

    def pass_on(t, carry):
        source = (y + near(t)) % ny
        slot = x * ny + source
        wait_bytes(ja.at[slot], r_ay.at[source])
        wait_bytes(jp.at[slot], r_py.at[source])
        forward(slot)
        return carry

    lax.fori_loop(0, ny - 1, pass_on, 0)
    v0 = build_rhs(targets[...], seeds[...])
    low = v0.astype(BF16).astype(F32)
    scale = amp[...]
    shift = noise[...]
    acc[...] = jnp.zeros_like(acc)

    wait_bytes(ip, r_pc)
    for c in range(nc):
        part = slice(c * LANES, (c + 1) * LANES)
        block = ip[c]
        n1, n2, n3 = pieces(minus_half_norm(block))
        weights[0:F, part] = block
        extra = jnp.where(sub < 3, 1.0, jnp.where(sub == 3, n1, jnp.where(sub == 4, n2, jnp.where(sub == 5, n3, 0.0))))
        weights[F:ROWS, part] = jnp.concatenate([extra, jnp.zeros_like(extra)], axis=0).astype(BF16)

    def first_pass(t, carry):
        g = (x + turn(t)) % nx

        @pl.when(t > 0)
        def _():
            wait_bytes(ja.at[pl.ds(g * ny, ny)], r_ax.at[g])
            wait_bytes(jp.at[pl.ds(g * ny, ny)], r_px.at[g])

        blocks, tails = [], []
        for k in range(ny):
            block = jp[g * ny + k]
            info = ja[g * ny + k]
            n1, n2, n3 = pieces(minus_half_norm(block))
            extra = jnp.where(sub == 0, n1, jnp.where(sub == 1, n2, jnp.where(sub == 2, n3, jnp.where(sub < 6, 1.0, 0.0))))
            blocks.append(block)
            tails.append(jnp.concatenate([extra, build_rhs(info[0:1], info[1:2])], axis=0).astype(BF16))
        tail = jnp.concatenate(tails, axis=1)
        block = jnp.concatenate([jnp.concatenate(blocks, axis=1), tail], axis=0)
        inner = lax.dot_general(block, weights[...], (((0,), (0,)), ((), ())), preferred_element_type=F32)
        kern = jnp.exp(inner).astype(BF16)
        tile[pl.ds(pl.multiple_of(g * group, group), group), :] = kern
        acc[...] += jnp.dot(tail, kern, preferred_element_type=F32)
        return carry

    lax.fori_loop(0, nx, first_pass, 0)

    to_cols((lambda peer: acc.at[pl.ds(RHS, RHS), pl.ds(pl.multiple_of(peer * LANES, LANES), LANES)],
             rs1.at[col], s_rs1, r_rs1))
    wait_bytes(ia, r_ac)
    for c in range(nc):
        v_i[:, c * LANES:(c + 1) * LANES] = build_rhs(ia[c, 0:1], ia[c, 1:2])
    low_i = v_i[...].astype(BF16).astype(F32)
    s1_msg[...] = as_row((
        rowsum(v0 * v0), scale * rowsum(low_i * acc[RHS:2 * RHS, :]) + rowsum(shift * low * low)))
    to_cols((lambda peer: s1_msg, s1_col.at[col], s_s1c, r_s1c))
    wait_bytes(rs1, r_rs1)
    q1 = scale * jnp.sum(rs1[...], axis=0) + shift * low
    q1_msg[...] = q1
    to_rows((q1_msg, j2.at[row], s_q1r, r_q1r.at[x]))
    wait_bytes(s1_col, r_s1c)
    s1_sum[...] = jnp.sum(s1_col[...], axis=0)
    to_rows((s1_sum, s1_row.at[row], s_s1r, r_s1r))
    to_cols((lambda peer: q1_msg, i2.at[col], s_q1c, r_q1c))

    wait_bytes(rs1.at[pl.ds(0, nc - 1)], s_rs1)
    acc[...] = jnp.zeros_like(acc)

    def second_pass(t, carry):
        g = (x + turn(t)) % nx
        wait_bytes(j2.at[pl.ds(g * ny, ny)], r_q1r.at[g])
        value = jnp.concatenate([j2[g * ny + k] for k in range(ny)], axis=1)
        high = value.astype(BF16).astype(F32)
        both = jnp.concatenate([high, value - high], axis=0).astype(BF16)
        acc[...] += jnp.dot(both, tile[pl.ds(pl.multiple_of(g * group, group), group), :],
                            preferred_element_type=F32)
        return carry

    lax.fori_loop(0, nx, second_pass, 0)
    wait_bytes(i2, r_q1c)
    wait_bytes(s1_row, r_s1r)
    total1 = jnp.sum(s1_row[...], axis=0)
    rr0 = from_row(total1, 0)
    curve1 = from_row(total1, 1)
    alpha1 = rr0 / curve1
    r1 = v0 - alpha1 * q1

    cross = jnp.zeros((RHS, LANES), F32)
    for c in range(nc):
        part = slice(c * LANES, (c + 1) * LANES)
        second = acc[0:RHS, part] + acc[RHS:2 * RHS, part]
        out2[c] = second
        cross = cross + (v_i[:, part] - alpha1 * i2[c]) * second
    s2_msg[...] = as_row((rowsum(scale * cross + shift * r1 * q1), rowsum(r1 * r1), rowsum(r1 * q1)))
    to_cols((lambda peer: s2_msg, s2_col.at[col], s_s2c, r_s2c))
    to_cols((lambda peer: out2.at[peer], rs2.at[col], s_rs2, r_rs2))
    wait_bytes(s2_col, r_s2c)
    s2_sum[...] = jnp.sum(s2_col[...], axis=0)
    to_rows((s2_sum, s2_row.at[row], s_s2r, r_s2r))
    wait_bytes(rs2, r_rs2)
    q2 = scale * jnp.sum(rs2[...], axis=0) + shift * q1

    wait_bytes(ip.at[pl.ds(0, nc - 1)], s_pc)
    wait_bytes(jp.at[pl.ds(0, ny - 1)], s_pr)
    wait_bytes(jp.at[pl.ds(0, nr - ny)], s_px)
    wait_bytes(ia.at[pl.ds(0, nc - 1)], s_ac)
    wait_bytes(ja.at[pl.ds(0, ny - 1)], s_ar)
    wait_bytes(ja.at[pl.ds(0, nr - ny)], s_ax)
    wait_bytes(s1_col.at[pl.ds(0, nc - 1)], s_s1c)
    wait_bytes(s1_row.at[pl.ds(0, nr - 1)], s_s1r)
    wait_bytes(j2.at[pl.ds(0, nr - 1)], s_q1r)
    wait_bytes(i2.at[pl.ds(0, nc - 1)], s_q1c)
    wait_bytes(s2_col.at[pl.ds(0, nc - 1)], s_s2c)
    wait_bytes(rs2.at[pl.ds(0, nc - 1)], s_rs2)
    wait_bytes(s2_row.at[pl.ds(0, nr - 1)], s_s2r)

    wait_bytes(s2_row, r_s2r)
    total2 = jnp.sum(s2_row[...], axis=0)
    r1q2, rr1, r1q1 = (from_row(total2, q) for q in range(3))
    beta = rr1 / rr0
    curve2 = (r1q1 - alpha1 * r1q2) + 2.0 * beta * r1q1 + beta * beta * curve1
    alpha2 = rr1 / curve2
    d2 = r1 + beta * v0
    image2 = (q1 - alpha1 * q2) + beta * q1
    both[0] = alpha1 * v0 + alpha2 * d2
    both[1] = r1 - alpha2 * image2


def solution(mesh):
    nr, nc = mesh.shape["row"], mesh.shape["col"]
    ny = 8 if nr % 8 == 0 else nr
    nx = nr // ny
    vmem = pl.BlockSpec(memory_space=pltpu.VMEM)
    anywhere = pl.BlockSpec(memory_space=pltpu.HBM)
    dma = pltpu.SemaphoreType.DMA

    def shards(points, inv_scale, amplitude, noise, targets, probe_seeds):
        out = jax.ShapeDtypeStruct((2, RHS, LANES), F32)
        line = pltpu.VMEM((1, LANES), F32)
        plane = pltpu.VMEM((RHS, LANES), F32)
        pair = pl.pallas_call(
            lambda *refs: body(nx, ny, nc, refs),
            out_shape=out,
            in_specs=[anywhere] * 6,
            out_specs=vmem,
            scratch_shapes=[
                pltpu.VMEM((F, LANES), BF16), pltpu.VMEM((1, F), F32), pltpu.VMEM((1, 1), F32),
                line, line, pltpu.VMEM((1, LANES), jnp.int32),
                pltpu.VMEM((F, LANES), BF16), pltpu.VMEM((2, LANES), F32),
                pltpu.VMEM((nr, F, LANES), BF16), pltpu.VMEM((nr, 2, LANES), F32),
                pltpu.VMEM((nc, F, LANES), BF16), pltpu.VMEM((nc, 2, LANES), F32),
                pltpu.VMEM((ROWS, nc * LANES), BF16), pltpu.VMEM((RHS, nc * LANES), F32),
                pltpu.VMEM((nr * LANES, nc * LANES), BF16), pltpu.VMEM((2 * RHS, nc * LANES), F32),
                pltpu.VMEM((nc, RHS, LANES), F32), line, pltpu.VMEM((nc, 1, LANES), F32), line,
                pltpu.VMEM((nr, 1, LANES), F32),
                plane, pltpu.VMEM((nr, RHS, LANES), F32), pltpu.VMEM((nc, RHS, LANES), F32),
                pltpu.VMEM((nc, RHS, LANES), F32),
                line, pltpu.VMEM((nc, 1, LANES), F32), pltpu.VMEM((nc, RHS, LANES), F32), line,
                pltpu.VMEM((nr, 1, LANES), F32),
                dma((6,)), dma, dma, dma, dma, dma((ny,)), dma((nx,)), dma, dma, dma, dma, dma((ny,)), dma((nx,)), dma, dma, dma, dma, dma, dma,
                dma, dma, dma, dma((nx,)), dma, dma, dma, dma, dma, dma,
            ],
            compiler_params=pltpu.CompilerParams(
                collective_id=0, has_side_effects=True, vmem_limit_bytes=48 * 2**20),
        )(points, inv_scale.reshape(1, F), amplitude.reshape(1, 1), noise.reshape(1, LANES),
          targets.reshape(1, LANES), probe_seeds.reshape(1, LANES))
        return pair[0], pair[1]

    spec = P(("row", "col"))
    both = P(None, ("row", "col"))
    return jax.shard_map(
        shards, mesh=mesh, in_specs=(both, P(), P(), spec, spec, spec),
        out_specs=(both, both), check_vma=False)
```

```python
import jax
import jax.numpy as jnp
from jax import lax
from jax.experimental import pallas as pl
from jax.experimental.pallas import tpu as pltpu
from jax.sharding import PartitionSpec as P

MESH = pl.DeviceIdType.MESH
F = 32
TAIL = 16
ROWS = F + TAIL
RHS = 8
LANES = 128
F32 = jnp.float32
BF16 = jnp.bfloat16


def pieces(value):
    first = value.astype(BF16).astype(F32)
    rest = value - first
    second = rest.astype(BF16).astype(F32)
    return first, second, rest - second


def wait_bytes(ref, sem):
    pltpu.make_async_copy(ref, ref, sem).wait()


def body(nx, ny, nc, refs):
    (points_in, inv_in, amp_in, noise_in, targets_in, seeds_in, both) = refs[:7]
    (points, inv, amp, noise, targets, seeds) = refs[7:13]
    (pts, aux, jp, ja, ip, ia, weights, v_i, tile, acc, rs1, s1_msg, s1_col, s1_sum, s1_row,
     q1_msg, j2, i2, out2, s2_msg, s2_col, rs2, s2_sum, s2_row) = refs[13:37]
    (in_sem, s_pc, s_pr, s_px, r_pc, r_py, r_px, s_ac, s_ar, s_ax, r_ac, r_ay, r_ax, s_rs1, r_rs1, s_s1c, r_s1c, s_s1r, r_s1r,
     s_q1c, s_q1r, r_q1c, r_q1r, s_s2c, r_s2c, s_rs2, r_rs2, s_s2r, r_s2r) = refs[37:]
    nr = nx * ny
    group = ny * LANES
    row = lax.axis_index("row")
    col = lax.axis_index("col")
    x = row // ny
    y = row % ny
    nz = nc // 2
    z = col // 2
    core = col % 2

    def turn(t):
        return (t * (7 - t) // 2) % 4 if nx == 4 else t

    def offset(t, n):
        half = (t + 1) // 2
        return (t % 2) * half + (1 - t % 2) * ((n - half) % n)

    def row_peer(k):
        far_y, far_x = ny - 1 - k // nx, nx - 1 - k % nx
        return ((x + offset(far_x, nx)) % nx) * ny + (y + offset(far_y, ny)) % ny

    def col_peer(k):
        far_z, far_core = nz - 1 - k // 2, 1 - k % 2
        return ((z + offset(far_z, nz)) % nz) * 2 + (core + far_core) % 2

    def row_peer_x(k):
        far_x, far_y = nx - 1 - k // ny, ny - 1 - k % ny
        return ((x + offset(far_x, nx)) % nx) * ny + (y + offset(far_y, ny)) % ny

    def row_peer_n(k):
        near_x, near_y = (k + 1) // ny, (k + 1) % ny
        return ((x + nx - turn(near_x)) % nx) * ny + (y + near_y) % ny

    def y_peer(k):
        return (x * ny + (y + k) % ny, col)

    def x_peer(k):
        return (((x + k) % nx) * ny + y, col)

    def near(t):
        half = t // 2 + 1
        return half + (t % 2) * (ny - 2 * half)

    def to_rows(*copies, peer_of=row_peer):
        for src, dst, send, recv in copies:
            pltpu.make_async_copy(src, dst, recv).start()

        def go(k, carry):
            peer = peer_of(k)
            for src, dst, send, recv in copies:
                pltpu.make_async_remote_copy(
                    src_ref=src, dst_ref=dst, send_sem=send, recv_sem=recv,
                    device_id=(peer, col), device_id_type=MESH,
                ).start()
            return carry

        lax.fori_loop(0, nr - 1, go, 0, unroll=True)

    def to_cols(*copies):
        for src_of, dst, send, recv in copies:
            pltpu.make_async_copy(src_of(col), dst, recv).start()

        def go(k, carry):
            peer = col_peer(k)
            for src_of, dst, send, recv in copies:
                pltpu.make_async_remote_copy(
                    src_ref=src_of(peer), dst_ref=dst, send_sem=send, recv_sem=recv,
                    device_id=(row, peer), device_id_type=MESH,
                ).start()
            return carry

        lax.fori_loop(0, nc - 1, go, 0, unroll=True)

    loads = [pltpu.make_async_copy(a, b, in_sem.at[n]) for n, (a, b) in enumerate((
        (points_in, points), (inv_in, inv), (targets_in, targets), (seeds_in, seeds),
        (noise_in, noise), (amp_in, amp)))]
    for load in loads:
        load.start()

    barrier = pltpu.get_barrier_semaphore()

    def greet(peer_of):
        def go(k, carry):
            pl.semaphore_signal(barrier, inc=1, device_id=peer_of(k), device_id_type=MESH)
            return carry

        return go

    lax.fori_loop(1, ny, greet(y_peer), 0)
    lax.fori_loop(1, nx, greet(x_peer), 0)
    lax.fori_loop(0, nc - 1, greet(lambda k: (row, col_peer(k))), 0)

    sub = lax.broadcasted_iota(jnp.int32, (RHS, LANES), 0)
    lane = lax.broadcasted_iota(jnp.int32, (RHS, LANES), 1)

    def build_rhs(target, seed):
        bits = (seed.astype(jnp.int32) >> jnp.maximum(sub - 1, 0)) & 1
        return jnp.where(sub == 0, target, (1 - 2 * bits).astype(F32))

    def minus_half_norm(block):
        values = block.astype(F32)
        return -0.5 * jnp.sum(values * values, axis=0, keepdims=True)

    def as_row(sums):
        spread = jnp.zeros((RHS, LANES), F32)
        for q, value in enumerate(sums):
            spread = spread + jnp.where(lane == q * RHS + sub, value, 0.0)
        return jnp.sum(spread, axis=0, keepdims=True)

    def from_row(total, q):
        return jnp.sum(jnp.where(lane == q * RHS + sub, total, 0.0), axis=1, keepdims=True)

    def rowsum(value):
        return jnp.sum(value, axis=1, keepdims=True)

    for load in loads:
        load.wait()
    eye = lax.broadcasted_iota(jnp.int32, (F, F), 0) == lax.broadcasted_iota(jnp.int32, (F, F), 1)
    factor = jnp.sum(jnp.where(eye, inv[...], 0.0), axis=1, keepdims=True)
    pts[...] = (points[...].astype(F32) * factor).astype(BF16)
    aux[0:1, :] = targets[...]
    aux[1:2, :] = seeds[...].astype(F32)

    pl.semaphore_wait(barrier, ny - 1 + nx - 1 + nc - 1)
    to_cols((lambda peer: pts, ip.at[col], s_pc, r_pc))

    def copy_to(device, src, dst, send, recv):
        pltpu.make_async_remote_copy(
            src_ref=src, dst_ref=dst, send_sem=send, recv_sem=recv,
            device_id=device, device_id_type=MESH,
        ).start()

    def forward(slot):
        def go(k, carry):
            copy_to(x_peer(k), ja.at[slot], ja.at[slot], s_ax, r_ax.at[x])
            copy_to(x_peer(k), jp.at[slot], jp.at[slot], s_px, r_px.at[x])
            return carry

        lax.fori_loop(1, nx, go, 0)

    def to_ring(t, carry):
        peer = y_peer(near(ny - 2 - t))
        copy_to(peer, aux, ja.at[row], s_ar, r_ay.at[y])
        copy_to(peer, pts, jp.at[row], s_pr, r_py.at[y])
        return carry

    lax.fori_loop(0, ny - 1, to_ring, 0)
    ja[row] = aux[...]
    jp[row] = pts[...]
    forward(row)
    to_cols((lambda peer: aux, ia.at[col], s_ac, r_ac))

    def pass_on(t, carry):
        source = (y + near(t)) % ny
        slot = x * ny + source
        wait_bytes(ja.at[slot], r_ay.at[source])
        wait_bytes(jp.at[slot], r_py.at[source])
        forward(slot)
        return carry

    lax.fori_loop(0, ny - 1, pass_on, 0)
    v0 = build_rhs(targets[...], seeds[...])
    low = v0.astype(BF16).astype(F32)
    scale = amp[...]
    shift = noise[...]
    acc[...] = jnp.zeros_like(acc)

    wait_bytes(ip, r_pc)
    for c in range(nc):
        part = slice(c * LANES, (c + 1) * LANES)
        block = ip[c]
        n1, n2, n3 = pieces(minus_half_norm(block))
        weights[0:F, part] = block
        extra = jnp.where(sub < 3, 1.0, jnp.where(sub == 3, n1, jnp.where(sub == 4, n2, jnp.where(sub == 5, n3, 0.0))))
        weights[F:ROWS, part] = jnp.concatenate([extra, jnp.zeros_like(extra)], axis=0).astype(BF16)

    def first_pass(t, carry):
        g = (x + turn(t)) % nx

        @pl.when(t > 0)
        def _():
            wait_bytes(ja.at[pl.ds(g * ny, ny)], r_ax.at[g])
            wait_bytes(jp.at[pl.ds(g * ny, ny)], r_px.at[g])

        blocks, tails = [], []
        for k in range(ny):
            block = jp[g * ny + k]
            info = ja[g * ny + k]
            n1, n2, n3 = pieces(minus_half_norm(block))
            extra = jnp.where(sub == 0, n1, jnp.where(sub == 1, n2, jnp.where(sub == 2, n3, jnp.where(sub < 6, 1.0, 0.0))))
            blocks.append(block)
            tails.append(jnp.concatenate([extra, build_rhs(info[0:1], info[1:2])], axis=0).astype(BF16))
        tail = jnp.concatenate(tails, axis=1)
        block = jnp.concatenate([jnp.concatenate(blocks, axis=1), tail], axis=0)
        inner = lax.dot_general(block, weights[...], (((0,), (0,)), ((), ())), preferred_element_type=F32)
        kern = jnp.exp(inner).astype(BF16)
        tile[pl.ds(pl.multiple_of(g * group, group), group), :] = kern
        acc[...] += jnp.dot(tail, kern, preferred_element_type=F32)
        return carry

    lax.fori_loop(0, nx, first_pass, 0)

    to_cols((lambda peer: acc.at[pl.ds(RHS, RHS), pl.ds(pl.multiple_of(peer * LANES, LANES), LANES)],
             rs1.at[col], s_rs1, r_rs1))
    wait_bytes(ia, r_ac)
    for c in range(nc):
        v_i[:, c * LANES:(c + 1) * LANES] = build_rhs(ia[c, 0:1], ia[c, 1:2])
    low_i = v_i[...].astype(BF16).astype(F32)
    s1_msg[...] = as_row((
        rowsum(v0 * v0), scale * rowsum(low_i * acc[RHS:2 * RHS, :]) + rowsum(shift * low * low)))
    to_cols((lambda peer: s1_msg, s1_col.at[col], s_s1c, r_s1c))
    wait_bytes(rs1, r_rs1)
    q1 = scale * jnp.sum(rs1[...], axis=0) + shift * low
    q1_msg[...] = q1
    to_rows((q1_msg, j2.at[row], s_q1r, r_q1r.at[x]))
    wait_bytes(s1_col, r_s1c)
    s1_sum[...] = jnp.sum(s1_col[...], axis=0)
    to_rows((s1_sum, s1_row.at[row], s_s1r, r_s1r))
    to_cols((lambda peer: q1_msg, i2.at[col], s_q1c, r_q1c))

    wait_bytes(rs1.at[pl.ds(0, nc - 1)], s_rs1)
    acc[...] = jnp.zeros_like(acc)

    def second_pass(t, carry):
        g = (x + turn(t)) % nx
        wait_bytes(j2.at[pl.ds(g * ny, ny)], r_q1r.at[g])
        value = jnp.concatenate([j2[g * ny + k] for k in range(ny)], axis=1)
        high = value.astype(BF16).astype(F32)
        both = jnp.concatenate([high, value - high], axis=0).astype(BF16)
        acc[...] += jnp.dot(both, tile[pl.ds(pl.multiple_of(g * group, group), group), :],
                            preferred_element_type=F32)
        return carry

    lax.fori_loop(0, nx, second_pass, 0)
    wait_bytes(i2, r_q1c)
    wait_bytes(s1_row, r_s1r)
    total1 = jnp.sum(s1_row[...], axis=0)
    rr0 = from_row(total1, 0)
    curve1 = from_row(total1, 1)
    alpha1 = rr0 / curve1
    r1 = v0 - alpha1 * q1

    cross = jnp.zeros((RHS, LANES), F32)
    for c in range(nc):
        part = slice(c * LANES, (c + 1) * LANES)
        second = acc[0:RHS, part] + acc[RHS:2 * RHS, part]
        out2[c] = second
        cross = cross + (v_i[:, part] - alpha1 * i2[c]) * second
    s2_msg[...] = as_row((rowsum(scale * cross + shift * r1 * q1), rowsum(r1 * r1), rowsum(r1 * q1)))
    to_cols((lambda peer: s2_msg, s2_col.at[col], s_s2c, r_s2c))
    to_cols((lambda peer: out2.at[peer], rs2.at[col], s_rs2, r_rs2))
    wait_bytes(s2_col, r_s2c)
    s2_sum[...] = jnp.sum(s2_col[...], axis=0)
    to_rows((s2_sum, s2_row.at[row], s_s2r, r_s2r))
    wait_bytes(rs2, r_rs2)
    q2 = scale * jnp.sum(rs2[...], axis=0) + shift * q1

    wait_bytes(ip.at[pl.ds(0, nc - 1)], s_pc)
    wait_bytes(jp.at[pl.ds(0, ny - 1)], s_pr)
    wait_bytes(jp.at[pl.ds(0, nr - ny)], s_px)
    wait_bytes(ia.at[pl.ds(0, nc - 1)], s_ac)
    wait_bytes(ja.at[pl.ds(0, ny - 1)], s_ar)
    wait_bytes(ja.at[pl.ds(0, nr - ny)], s_ax)
    wait_bytes(s1_col.at[pl.ds(0, nc - 1)], s_s1c)
    wait_bytes(s1_row.at[pl.ds(0, nr - 1)], s_s1r)
    wait_bytes(j2.at[pl.ds(0, nr - 1)], s_q1r)
    wait_bytes(i2.at[pl.ds(0, nc - 1)], s_q1c)
    wait_bytes(s2_col.at[pl.ds(0, nc - 1)], s_s2c)
    wait_bytes(rs2.at[pl.ds(0, nc - 1)], s_rs2)
    wait_bytes(s2_row.at[pl.ds(0, nr - 1)], s_s2r)

    wait_bytes(s2_row, r_s2r)
    total2 = jnp.sum(s2_row[...], axis=0)
    r1q2, rr1, r1q1 = (from_row(total2, q) for q in range(3))
    beta = rr1 / rr0
    curve2 = (r1q1 - alpha1 * r1q2) + 2.0 * beta * r1q1 + beta * beta * curve1
    alpha2 = rr1 / curve2
    d2 = r1 + beta * v0
    image2 = (q1 - alpha1 * q2) + beta * q1
    both[0] = alpha1 * v0 + alpha2 * d2
    both[1] = r1 - alpha2 * image2


def solution(mesh):
    nr, nc = mesh.shape["row"], mesh.shape["col"]
    ny = 8 if nr % 8 == 0 else nr
    nx = nr // ny
    vmem = pl.BlockSpec(memory_space=pltpu.VMEM)
    anywhere = pl.BlockSpec(memory_space=pltpu.HBM)
    dma = pltpu.SemaphoreType.DMA

    def shards(points, inv_scale, amplitude, noise, targets, probe_seeds):
        out = jax.ShapeDtypeStruct((2, RHS, LANES), F32)
        line = pltpu.VMEM((1, LANES), F32)
        plane = pltpu.VMEM((RHS, LANES), F32)
        pair = pl.pallas_call(
            lambda *refs: body(nx, ny, nc, refs),
            out_shape=out,
            in_specs=[anywhere] * 6,
            out_specs=vmem,
            scratch_shapes=[
                pltpu.VMEM((F, LANES), BF16), pltpu.VMEM((1, F), F32), pltpu.VMEM((1, 1), F32),
                line, line, pltpu.VMEM((1, LANES), jnp.int32),
                pltpu.VMEM((F, LANES), BF16), pltpu.VMEM((2, LANES), F32),
                pltpu.VMEM((nr, F, LANES), BF16), pltpu.VMEM((nr, 2, LANES), F32),
                pltpu.VMEM((nc, F, LANES), BF16), pltpu.VMEM((nc, 2, LANES), F32),
                pltpu.VMEM((ROWS, nc * LANES), BF16), pltpu.VMEM((RHS, nc * LANES), F32),
                pltpu.VMEM((nr * LANES, nc * LANES), BF16), pltpu.VMEM((2 * RHS, nc * LANES), F32),
                pltpu.VMEM((nc, RHS, LANES), F32), line, pltpu.VMEM((nc, 1, LANES), F32), line,
                pltpu.VMEM((nr, 1, LANES), F32),
                plane, pltpu.VMEM((nr, RHS, LANES), F32), pltpu.VMEM((nc, RHS, LANES), F32),
                pltpu.VMEM((nc, RHS, LANES), F32),
                line, pltpu.VMEM((nc, 1, LANES), F32), pltpu.VMEM((nc, RHS, LANES), F32), line,
                pltpu.VMEM((nr, 1, LANES), F32),
                dma((6,)), dma, dma, dma, dma, dma((ny,)), dma((nx,)), dma, dma, dma, dma, dma((ny,)), dma((nx,)), dma, dma, dma, dma, dma, dma,
                dma, dma, dma, dma((nx,)), dma, dma, dma, dma, dma, dma,
            ],
            compiler_params=pltpu.CompilerParams(
                collective_id=0, has_side_effects=True, vmem_limit_bytes=48 * 2**20),
        )(points, inv_scale.reshape(1, F), amplitude.reshape(1, 1), noise.reshape(1, LANES),
          targets.reshape(1, LANES), probe_seeds.reshape(1, LANES))
        return pair[0], pair[1]

    spec = P(("row", "col"))
    both = P(None, ("row", "col"))
    return jax.shard_map(
        shards, mesh=mesh, in_specs=(both, P(), P(), spec, spec, spec),
        out_specs=(both, both), check_vma=False)
```
